256 devices in a mesh: ens: 4 (over x_hi, core), date: 8 (over z), pix: 8 (over y, x_lo).
Axes of the slice: x: 4 (x_hi: 2, x_lo: 2; x = x_hi * 2 + x_lo), y: 4, z: 8, core: 2. Of those that a mesh axis runs over, the one named last changes fastest.
Arguments:
- hindcast_runs: bfloat16 [4, 104, 4, 46, 8192], P('ens', 'date', None, None, 'pix'), may hold values from -16 to 16
- init_calendar_ordinal: int32 [104], replicated, may hold values from 0 to 367, as said below
- prediction_init_position: int32 [1], replicated, may hold values from 0 to 103
- horizon_sevenfold_bin: int32 [46], replicated, may hold values from 0 to 6, never falling along the last dimension, each value on 1 to 8 neighbouring positions
- prediction_runs: bfloat16 [11, 4, 46, 8192], P(None, 'ens', None, ('pix', 'date')), may hold values from -16 to 16
Outputs:
- smoothed_norm: float32 [104, 4, 46, 8192], P('date', 'ens', None, 'pix')
- anomalies: float32 [7, 4, 8192], P(None, 'ens', ('pix', 'date'))
The draws below stay inside these ranges and needn't reach their ends.
Inputs may be any that keep to these rules, and one draw needn't show every extreme that they name: `init_calendar_ordinal`: strictly increasing; the first is a day of 0 to 6, consecutive start dates lie 3 or 4 days apart, the last lies 3 or 4 days before the first plus 364, and half of these 104 gaps are 4 days. `horizon_sevenfold_bin`: Non-decreasing; every bin of 0 to 6 holds 1 to 8 consecutive leads.
All inputs are finite; a program needn't handle non-finite values.
Results may differ from the reference program's by a relative error of at most 0.01.
Values may be sent and summed in bfloat16 or wider, within the bound.
No kernel may reach another device: no remote copies, remote signals or barrier semaphores. Data moves between devices by JAX's collectives and lax.ppermute only.
A program may use at most 128 MiB of HBM per device.

```python
import math
import jax
import jax.numpy as jnp
import numpy as np
from jax import lax

MEMBER_YEARS = 4
INIT_MOMENTS = 104
CYCLE = 364
QUANTITY_KINDS = 4
HORIZON_STEPS = 46
TILE_CELLS = 8192
PREDICTION_RUNS = 11
WEEKS = 7


def draw_init_calendar_ordinal(key, part):
    key = jax.random.fold_in(key, 7)
    order_key, start_key = jax.random.split(key)
    order = jax.random.permutation(order_key, INIT_MOMENTS)
    gap_days = 3 + (order < INIT_MOMENTS // 2).astype(jnp.int32)
    start_day = jax.random.randint(start_key, (), 0, 7)
    return (start_day + jnp.cumsum(gap_days) - gap_days).astype(jnp.int32)


def block_levels(key, shape, cuts, low, high):
    def one(dim, shards_of):
        draws = jax.random.uniform(jax.random.fold_in(jax.random.fold_in(key, 6), dim), (shards_of,), jnp.float32, low / len(cuts), high / len(cuts))
        return jnp.repeat(jnp.exp(draws), shape[dim] // shards_of).reshape((-1,) + (1,) * (len(shape) - dim - 1))

    level = one(*cuts[0])
    for cut in cuts[1:]:
        level = level * one(*cut)
    return level


def split_up(number_of, total, limit, skew):
    portions = [(1 << 20) // math.isqrt(rank ** skew) + 1 for rank in range(2, number_of + 1)]
    rest, holding = total - limit - (number_of - 1), [1] * (number_of - 1)
    while rest > 0:
        candidates = [i for i in range(number_of - 1) if holding[i] < limit]
        whole, left = sum([portions[i] for i in candidates]), rest
        for i in candidates:
            addition = min(limit - holding[i], max(1, left * portions[i] // whole), rest)
            holding[i] = holding[i] + addition
            rest = rest - addition
    return np.array([limit] + holding)


def uneven(own_key, amount, total, limit, skew):
    if amount == 2:
        one = jax.random.randint(own_key, (), max(1, total - limit), min(limit, total - 1) + 1)
        return jnp.stack([one, total - one])
    lengths = jnp.asarray(split_up(amount, total, limit, skew), jnp.int32)
    twos = (amount - 1) // 2
    giver, taker = lengths[1:1 + 2 * twos:2], lengths[2:2 + 2 * twos:2]
    margin = jnp.minimum(giver - 1, limit - taker)
    passed = jax.random.randint(jax.random.fold_in(own_key, 1), (twos,), 0, 1 << 20) % (margin + 1)
    lengths = lengths.at[1:1 + 2 * twos:2].set(giver - passed).at[2:2 + 2 * twos:2].set(taker + passed)
    return lengths[jax.random.permutation(jax.random.fold_in(own_key, 2), amount)]


def centred(stream_key, shape, scale, bound, shards=(), held_as=jnp.bfloat16):
    factor_of = block_levels(stream_key, shape, shards, -0.22, 0.18) if shards else 1.0
    entries = jax.random.normal(stream_key, shape, jnp.float32) * scale * factor_of
    return jnp.minimum(jnp.maximum(entries, -bound), bound).astype(held_as)


def setup_inputs(seed: int = 0) -> dict:
    key_list = jax.random.split(jax.random.key(seed), 6)
    return {
        "hindcast_runs": centred(key_list[0], (MEMBER_YEARS, INIT_MOMENTS, QUANTITY_KINDS, HORIZON_STEPS, TILE_CELLS), 3.0, 16.0, ((0, 4), (1, 8), (4, 8))),
        "init_calendar_ordinal": draw_init_calendar_ordinal(jax.random.fold_in(key_list[5], 71), 0),
        "prediction_init_position": jax.random.randint(key_list[2], (1,), 0, INIT_MOMENTS).astype(jnp.int32),
        "horizon_sevenfold_bin": jnp.searchsorted(jnp.cumsum(uneven(key_list[3], WEEKS, HORIZON_STEPS, 8, 0)), jnp.arange(HORIZON_STEPS), side="right").astype(jnp.int32),
        "prediction_runs": centred(key_list[4], (PREDICTION_RUNS, QUANTITY_KINDS, HORIZON_STEPS, TILE_CELLS), 3.0, 16.0, ((1, 4), (3, 64))),
    }


def lead_smoother(length):
    positions = jnp.arange(length)
    distance = jnp.abs(positions[:, None] - positions[None, :])
    smoother = jnp.where(distance == 0, 2.0, jnp.where(distance == 1, 1.0, 0.0)).astype(jnp.float32)
    return smoother / jnp.sum(smoother, 1, keepdims=True)


def gap_weight(earlier, later, cycle_days):
    gap_days = jnp.mod(later - earlier, cycle_days)
    return jnp.maximum(8 - gap_days, 0).astype(jnp.float32)


def reference(hindcast_runs, init_calendar_ordinal, prediction_init_position, horizon_sevenfold_bin, prediction_runs):
    def accumulate(running, member_block):
        return running + member_block.astype(jnp.float32), None

    member_sum = lax.scan(accumulate, jnp.zeros(hindcast_runs.shape[1:], jnp.float32), hindcast_runs)[0]
    date_mean = 8.0 * member_sum
    weight_sum = jnp.full((INIT_MOMENTS,), 8.0, jnp.float32)
    for offset in (1, 2):
        forward = gap_weight(init_calendar_ordinal, jnp.roll(init_calendar_ordinal, -offset), CYCLE)
        backward = gap_weight(jnp.roll(init_calendar_ordinal, offset), init_calendar_ordinal, CYCLE)
        date_mean = date_mean + forward[:, None, None, None] * jnp.roll(member_sum, -offset, 0)
        date_mean = date_mean + backward[:, None, None, None] * jnp.roll(member_sum, offset, 0)
        weight_sum = weight_sum + forward + backward
    date_mean = date_mean / (MEMBER_YEARS * weight_sum)[:, None, None, None]
    smoothed_norm = jnp.einsum("ml,svlp->svmp", lead_smoother(HORIZON_STEPS), date_mean, precision=lax.Precision.HIGHEST)
    runs_centroid = jnp.mean(prediction_runs.astype(jnp.float32), 0)
    present_norm = lax.dynamic_index_in_dim(smoothed_norm, prediction_init_position[0], 0, keepdims=False)
    week_table = (horizon_sevenfold_bin[None, :] == jnp.arange(WEEKS, dtype=jnp.int32)[:, None]).astype(jnp.float32)
    bin_count = jnp.sum(week_table, 1)
    anomalies = jnp.einsum("wl,vlp->wvp", week_table, runs_centroid - present_norm, precision=lax.Precision.HIGHEST)
    anomalies = anomalies / bin_count[:, None, None]
    return smoothed_norm, anomalies
```

```python
import jax
import jax.numpy as jnp
from jax import lax
from jax.sharding import PartitionSpec as P

WEEKS = 7
SCALE = 512.0


def core_swap(block):
    return lax.ppermute(block, "ens", [(0, 1), (1, 0), (2, 3), (3, 2)])


def chip_swap(block):
    return lax.ppermute(block, "ens", [(0, 2), (1, 3), (2, 0), (3, 1)])


def date_shift(block, step):
    count = lax.axis_size("date")
    return lax.ppermute(block, "date", [(i, (i + step) % count) for i in range(count)])


def date_weights(days, cycle_days):
    columns = []
    for k in (-2, -1, 0, 1, 2):
        if k == 0:
            columns.append(jnp.full(days.shape, 8.0, jnp.float32))
            continue
        other = jnp.roll(days, -k)
        gap = jnp.mod(other - days if k > 0 else days - other, cycle_days)
        columns.append(jnp.maximum(8 - gap, 0).astype(jnp.float32))
    table = jnp.stack(columns, 1)
    return table / jnp.sum(table, 1, keepdims=True)


def smooth_leads(field, axis):
    length = field.shape[axis]
    shape = [1] * field.ndim
    shape[axis] = length
    positions = jnp.arange(length).reshape(shape)
    pads = [(0, 0)] * field.ndim
    pads[axis] = (1, 1)
    padded = jnp.pad(field, pads)
    before = lax.slice_in_dim(padded, 0, length, axis=axis)
    after = lax.slice_in_dim(padded, 2, length + 2, axis=axis)
    inverse = jnp.where((positions == 0) | (positions == length - 1), 1.0 / 3.0, 0.25)
    return (2.0 * field + before + after) * inverse.astype(jnp.float32)


def per_device(
    hindcast_runs,
    init_calendar_ordinal,
    prediction_init_position,
    horizon_sevenfold_bin,
    prediction_runs,
):
    runs = hindcast_runs[0]
    rows, kinds, leads, cells = runs.shape
    dates = rows * lax.axis_size("date")
    members = lax.axis_size("ens")
    cycle_days = 7 * dates // 2
    ens = lax.axis_index("ens")
    date = lax.axis_index("date")
    core = ens % 2
    half = ens // 2

    def of_kind(block, kind):
        return lax.dynamic_index_in_dim(block, kind, 1, keepdims=False)

    edge = [(0, 2), (rows - 2, rows)]
    inner = [(2, rows - 2)]

    def part(kind, spans):
        pieces = [of_kind(runs[a:b], kind) for a, b in spans]
        return pieces[0] if len(pieces) == 1 else jnp.concatenate(pieces, 0)

    def member_sum(spans):
        for_sibling = core_swap(part(2 * (1 - half) + 1 - core, spans))
        partial = part(2 * (1 - half) + core, spans).astype(jnp.float32) + for_sibling.astype(
            jnp.float32
        )
        arrived = chip_swap((partial * SCALE).astype(jnp.float16))
        from_sibling = core_swap(part(2 * half + 1 - core, spans))
        own = part(ens, spans).astype(jnp.float32) + from_sibling.astype(jnp.float32)
        return own + arrived.astype(jnp.float32) * (1.0 / SCALE)

    edges = member_sum(edge)
    middle = member_sum(inner)
    packed = (edges * SCALE).astype(jnp.float16)
    below = date_shift(packed[2:], 1).astype(jnp.float32) * (1.0 / SCALE)
    above = date_shift(packed[:2], -1).astype(jnp.float32) * (1.0 / SCALE)
    widened = jnp.concatenate([below, edges[:2], middle, edges[2:], above], 0)

    weights = date_weights(init_calendar_ordinal, cycle_days)
    own_weights = lax.dynamic_slice_in_dim(weights, date * rows, rows, 0) * (1.0 / members)
    mean = own_weights[:, 0, None, None] * widened[:rows]
    for k in range(1, 5):
        mean = mean + own_weights[:, k, None, None] * widened[k : k + rows]
    smoothed_norm = smooth_leads(mean, 1)[:, None]

    position = prediction_init_position[0]
    row_weights = lax.dynamic_index_in_dim(weights, position, 0, keepdims=False) * (1.0 / members)
    own_dates = date * rows + jnp.arange(rows)
    offsets = jnp.mod(own_dates - position + 2, dates)
    shares = jnp.sum(
        jnp.where(offsets[:, None] == jnp.arange(5)[None, :], row_weights[None, :], 0.0), 1
    )
    week_table = (
        horizon_sevenfold_bin[None, :] == jnp.arange(WEEKS, dtype=jnp.int32)[:, None]
    ).astype(jnp.float32)
    week_mean = week_table / jnp.sum(week_table, 1, keepdims=True)
    climate = jnp.sum(runs.astype(jnp.float32) * shares[:, None, None, None], 0)
    climate = smooth_leads(climate, 1)
    highest = lax.Precision.HIGHEST
    weekly = jnp.einsum("wl,vlp->vwp", week_mean, climate, precision=highest)
    slots = lax.axis_size("date")
    weekly = weekly.reshape(kinds, WEEKS, slots, cells // slots).transpose(0, 2, 1, 3)
    weekly = weekly.reshape(kinds * slots, WEEKS, cells // slots)
    weekly = lax.psum_scatter(weekly, ("ens", "date"), scatter_dimension=0)
    centroid = jnp.sum(prediction_runs[:, 0].astype(jnp.float32), 0) * (
        1.0 / prediction_runs.shape[0]
    )
    anomalies = jnp.einsum("wl,lp->wp", week_mean, centroid, precision=highest) - weekly
    return smoothed_norm, anomalies[:, None]


def solution(mesh):
    return jax.shard_map(
        per_device,
        mesh=mesh,
        in_specs=(
            P("ens", "date", None, None, "pix"),
            P(),
            P(),
            P(),
            P(None, "ens", None, ("pix", "date")),
        ),
        out_specs=(P("date", "ens", None, "pix"), P(None, "ens", ("pix", "date"))),
        check_vma=False,
    )
```

```python
import functools

import jax
import jax.numpy as jnp
from jax import lax
from jax.experimental import pallas as pl
from jax.experimental.pallas import tpu as pltpu
from jax.sharding import PartitionSpec as P

WEEKS = 7
LANES = 128
TILE = 8
SCALE = 512.0
MIB = 1024 * 1024


def core_swap(block):
    return lax.ppermute(block, "ens", [(0, 1), (1, 0), (2, 3), (3, 2)])


def chip_swap(block):
    return lax.ppermute(block, "ens", [(0, 2), (1, 3), (2, 0), (3, 1)])


def date_shift(block, step):
    count = lax.axis_size("date")
    return lax.ppermute(block, "date", [(i, (i + step) % count) for i in range(count)])


def split_kernel(kinds, leads, roles, ens_ref, runs_ref, *rest):
    outs, wide = rest[:-1], rest[-1]
    ens = ens_ref[0]
    core, half = ens % 2, ens // 2
    wide[...] = runs_ref[...].astype(jnp.float32)
    for (other_half, other_core), out in zip(roles, outs):
        kind = 2 * (1 - half if other_half else half) + (1 - core if other_core else core)
        for lead in range(0, leads, 2):
            picked = wide[pl.ds(lead * TILE * kinds + kind, 2 * TILE, stride=kinds), :]
            out[lead * TILE : (lead + 2) * TILE, :] = picked.astype(jnp.bfloat16)


def split_kinds(flat, ens, kinds, leads, roles, count, row_of):
    block = leads * TILE
    shape = jax.ShapeDtypeStruct((count * block, LANES), jnp.bfloat16)
    outs = pl.pallas_call(
        functools.partial(split_kernel, kinds, leads, roles),
        grid_spec=pltpu.PrefetchScalarGridSpec(
            num_scalar_prefetch=1,
            grid=(count,),
            in_specs=[pl.BlockSpec((block * kinds, LANES), lambda i, _: (row_of(i), 0))],
            out_specs=[pl.BlockSpec((block, LANES), lambda i, _: (i, 0))] * len(roles),
            scratch_shapes=[pltpu.VMEM((block * kinds, LANES), jnp.float32)],
        ),
        out_shape=[shape] * len(roles),
        cost_estimate=pl.CostEstimate(
            flops=0, transcendentals=0, bytes_accessed=count * block * LANES * 2 * (kinds + len(roles))
        ),
        compiler_params=pltpu.CompilerParams(vmem_limit_bytes=56 * MIB),
    )(ens, flat)
    return list(outs)


def smooth_kernel(leads, places, rows, aliased, weight_ref, *refs):
    sums = refs[: -3 - aliased]
    out_hbm, done, sem = refs[-3:]

    def tile(date, lead):
        which, place = places[date]
        start = (place * leads + lead) * TILE
        return sums[which][start : start + TILE, :]

    copies = []
    for slot, row in enumerate(rows):
        weight = [weight_ref[row, k] for k in range(5)]

        def mean(lead):
            value = weight[0] * tile(row - 2, lead)
            for k in range(1, 5):
                value = value + weight[k] * tile(row - 2 + k, lead)
            return value

        before, here = None, mean(0)
        for lead in range(leads):
            after = mean(lead + 1) if lead + 1 < leads else None
            value = here + here
            for beside in (before, after):
                if beside is not None:
                    value = value + beside
            edge = before is None or after is None
            done[slot, lead * TILE : (lead + 1) * TILE, :] = value * (1.0 / 3.0 if edge else 0.25)
            before, here = here, after
        copy = pltpu.make_async_copy(done.at[slot], out_hbm.at[row], sem.at[slot])
        copy.start()
        copies.append(copy)
    for copy in copies:
        copy.wait()


def smooth_rows(weights, sums, places, rows, leads, total_rows, into=None):
    vmem = pl.BlockSpec(memory_space=pltpu.VMEM)
    smem = pl.BlockSpec(memory_space=pltpu.SMEM)
    hbm = pl.BlockSpec(memory_space=pl.ANY)
    aliased = 0 if into is None else 1
    operands = [weights, *sums] + ([into] if aliased else [])
    return pl.pallas_call(
        functools.partial(smooth_kernel, leads, places, rows, aliased),
        in_specs=[smem] + [vmem] * len(sums) + [hbm] * aliased,
        out_specs=hbm,
        out_shape=jax.ShapeDtypeStruct((total_rows, leads * TILE, LANES), jnp.float32),
        scratch_shapes=[
            pltpu.VMEM((len(rows), leads * TILE, LANES), jnp.float32),
            pltpu.SemaphoreType.DMA((len(rows),)),
        ],
        input_output_aliases={len(operands) - 1: 0} if aliased else {},
        compiler_params=pltpu.CompilerParams(vmem_limit_bytes=32 * MIB),
    )(*operands)


def weekly_one_kernel(leads, rows_of, share_ref, table_ref, *refs):
    pairs, out, total = refs[:-2], refs[-2], refs[-1]
    block = leads * TILE
    total[...] = jnp.zeros_like(total)
    for index, rows in enumerate(rows_of):
        first, second = pairs[2 * index], pairs[2 * index + 1]
        for place, row in enumerate(rows):

            @pl.when(share_ref[row] != 0.0)
            def _(first=first, second=second, place=place, row=row):
                span = slice(place * block, (place + 1) * block)
                both = first[span, :].astype(jnp.float32) + second[span, :].astype(jnp.float32)
                total[...] += share_ref[row] * both

    for week in range(WEEKS):
        mean = jnp.zeros((TILE, LANES), jnp.float32)
        for lead in range(leads):
            mean = mean + table_ref[week, lead] * total[lead * TILE : (lead + 1) * TILE, :]
        out[week * TILE : (week + 1) * TILE, :] = mean


def weekly_one(shares, table, leads, rows_of, pairs):
    vmem = pl.BlockSpec(memory_space=pltpu.VMEM)
    smem = pl.BlockSpec(memory_space=pltpu.SMEM)
    return pl.pallas_call(
        functools.partial(weekly_one_kernel, leads, rows_of),
        in_specs=[smem, smem] + [vmem] * len(pairs),
        out_specs=vmem,
        out_shape=jax.ShapeDtypeStruct((WEEKS * TILE, LANES), jnp.float32),
        scratch_shapes=[pltpu.VMEM((leads * TILE, LANES), jnp.float32)],
        compiler_params=pltpu.CompilerParams(vmem_limit_bytes=32 * MIB),
    )(shares, table, *pairs)


def date_weights(days, cycle_days):
    columns = []
    for k in (-2, -1, 0, 1, 2):
        if k == 0:
            columns.append(jnp.full(days.shape, 8.0, jnp.float32))
            continue
        other = jnp.roll(days, -k)
        gap = jnp.mod(other - days if k > 0 else days - other, cycle_days)
        columns.append(jnp.maximum(8 - gap, 0).astype(jnp.float32))
    table = jnp.stack(columns, 1)
    return table / jnp.sum(table, 1, keepdims=True)


def lead_smoother(length):
    positions = jnp.arange(length)
    distance = jnp.abs(positions[:, None] - positions[None, :])
    smoother = jnp.where(distance == 0, 2.0, jnp.where(distance == 1, 1.0, 0.0))
    smoother = smoother.astype(jnp.float32)
    return smoother / jnp.sum(smoother, 1, keepdims=True)


def per_device(
    hindcast_runs,
    init_calendar_ordinal,
    prediction_init_position,
    horizon_sevenfold_bin,
    prediction_runs,
):
    highest = lax.Precision.HIGHEST
    _, rows, kinds, leads, cells = hindcast_runs.shape
    slots = lax.axis_size("date")
    dates = rows * slots
    members = lax.axis_size("ens")
    cycle_days = 7 * dates // 2
    block = leads * TILE
    ens = lax.axis_index("ens").astype(jnp.int32)
    date = lax.axis_index("date").astype(jnp.int32)
    ens_operand = ens.reshape(1)

    flat = hindcast_runs.reshape(rows, kinds, leads, TILE, LANES)
    flat = flat.transpose(0, 2, 3, 1, 4).reshape(rows * leads * TILE * kinds, LANES)

    last = 2
    chunks = [
        [0, 1, rows - 2, rows - 1],
        list(range(2, rows - 2 - last)),
        list(range(rows - 2 - last, rows - 2)),
    ]
    row_maps = [
        lambda i: jnp.where(i < 2, i, i + rows - 4),
        lambda i: i + chunks[1][0],
        lambda i: i + chunks[2][0],
    ]
    roles = [(True, True), (True, False)]
    split_x = functools.partial(
        split_kinds, ens=ens_operand, kinds=kinds, leads=leads, roles=roles
    )

    def partial_sum(mine, other):
        return ((mine.astype(jnp.float32) + other.astype(jnp.float32)) * SCALE).astype(jnp.float16)

    sent, got, packed = [], [], []
    sent.append(split_x(flat, count=len(chunks[0]), row_of=row_maps[0]))
    got.append(core_swap(sent[0][0]))
    flat_1, *sent[0] = lax.optimization_barrier((flat, *sent[0]))
    sent.append(split_x(flat_1, count=len(chunks[1]), row_of=row_maps[1]))
    got.append(core_swap(sent[1][0]))
    mine, sent[1][1] = lax.optimization_barrier((sent[0][1], sent[1][1]))
    packed.append(partial_sum(mine, got[0]))
    flat_2, packed[0] = lax.optimization_barrier((flat, packed[0]))
    sent.append(split_x(flat_2, count=len(chunks[2]), row_of=row_maps[2]))
    got.append(core_swap(sent[2][0]))
    mine, sent[2][1] = lax.optimization_barrier((sent[1][1], sent[2][1]))
    packed.append(partial_sum(mine, got[1]))
    flat_3, packed[1] = lax.optimization_barrier((flat, packed[1]))
    theirs, own = split_kinds(
        flat_3, ens_operand, kinds, leads, [(False, True), (False, False)], rows, lambda i: i
    )
    own_got = core_swap(theirs)
    mine, own = lax.optimization_barrier((sent[2][1], own))
    packed.append(partial_sum(mine, got[2]))
    (
        packed[2],
        init_calendar_ordinal,
        prediction_init_position,
        horizon_sevenfold_bin,
        prediction_runs,
    ) = lax.optimization_barrier(
        (
            packed[2],
            init_calendar_ordinal,
            prediction_init_position,
            horizon_sevenfold_bin,
            prediction_runs,
        )
    )
    arrived = [chip_swap(block) for block in packed]

    def local_sum(first, count, packed):
        span = slice(first * block, (first + count) * block)
        pair = own[span].astype(jnp.float32) + own_got[span].astype(jnp.float32)
        return pair + packed.astype(jnp.float32) * (1.0 / SCALE)

    low = local_sum(0, 2, arrived[0][: 2 * block])
    high = local_sum(rows - 2, 2, arrived[0][2 * block :])
    below = date_shift(high, 1)
    above = date_shift(low, -1)
    middle = local_sum(chunks[1][0], len(chunks[1]), arrived[1])
    final = local_sum(chunks[2][0], len(chunks[2]), arrived[2])

    weights = date_weights(init_calendar_ordinal, cycle_days)
    own_weights = lax.dynamic_slice_in_dim(weights, date * rows, rows, 0) * (1.0 / members)
    places = {-2: (0, 0), -1: (0, 1), 0: (1, 0), 1: (1, 1)}
    places |= {row: (2, i) for i, row in enumerate(chunks[1])}
    places |= {rows - 2: (3, 0), rows - 1: (3, 1), rows: (4, 0), rows + 1: (4, 1)}
    ready = chunks[1][-1] - 1
    smoothed = smooth_rows(
        own_weights, [below, low, middle], places, list(range(ready)), leads, rows
    )
    places |= {row: (5, i) for i, row in enumerate(chunks[2])}
    smoothed = smooth_rows(
        own_weights,
        [below, low, middle, high, above, final],
        places,
        list(range(ready, rows)),
        leads,
        rows,
        smoothed,
    )
    smoothed_norm = smoothed.reshape(rows, 1, leads, cells)

    position = prediction_init_position[0]
    row_weights = lax.dynamic_index_in_dim(weights, position, 0, keepdims=False) * (1.0 / members)
    offsets = jnp.mod(date * rows + jnp.arange(rows) - position + 2, dates)
    shares = jnp.sum(
        jnp.where(offsets[:, None] == jnp.arange(5)[None, :], row_weights[None, :], 0.0), 1
    )
    week_table = (
        horizon_sevenfold_bin[None, :] == jnp.arange(WEEKS, dtype=jnp.int32)[:, None]
    ).astype(jnp.float32)
    week_mean = week_table / jnp.sum(week_table, 1, keepdims=True)
    climate_table = jnp.matmul(week_mean, lead_smoother(leads), precision=highest)
    pairs = []
    for (_, mine), other in zip(sent, got):
        pairs += [mine, other]
    weekly_sent = weekly_one(shares, climate_table, leads, chunks, pairs)
    weekly_own = weekly_one(shares, climate_table, leads, [list(range(rows))], [own, own_got])
    weekly = weekly_own + chip_swap(weekly_sent)
    weekly = weekly.reshape(WEEKS, slots, LANES).transpose(1, 0, 2)
    step = slots // 2
    while step:
        upper = (date // step) % 2
        give = lax.dynamic_slice_in_dim(weekly, (1 - upper) * step, step, 0)
        keep = lax.dynamic_slice_in_dim(weekly, upper * step, step, 0)
        weekly = keep + lax.ppermute(give, "date", [(i, i ^ step) for i in range(slots)])
        step //= 2
    centroid = jnp.sum(prediction_runs[:, 0].astype(jnp.float32), 0) * (
        1.0 / prediction_runs.shape[0]
    )
    anomalies = jnp.einsum("wl,lp->wp", week_mean, centroid, precision=highest) - weekly[0]
    return smoothed_norm, anomalies[:, None]


def solution(mesh):
    return jax.shard_map(
        per_device,
        mesh=mesh,
        in_specs=(
            P("ens", "date", None, None, "pix"),
            P(),
            P(),
            P(),
            P(None, "ens", None, ("pix", "date")),
        ),
        out_specs=(P("date", "ens", None, "pix"), P(None, "ens", ("pix", "date"))),
        check_vma=False,
    )
```

```python
import functools

import jax
import jax.numpy as jnp
from jax import lax
from jax.experimental import pallas as pl
from jax.experimental.pallas import tpu as pltpu
from jax.sharding import PartitionSpec as P

WEEKS = 7
LANES = 128
TILE = 8
SCALE = 512.0
MIB = 1024 * 1024
SMALL = pl.CostEstimate(flops=1, transcendentals=0, bytes_accessed=1)


def core_swap(block):
    return lax.ppermute(block, "ens", [(0, 1), (1, 0), (2, 3), (3, 2)])


def chip_swap(block):
    return lax.ppermute(block, "ens", [(0, 2), (1, 3), (2, 0), (3, 1)])


def date_shift(block, step):
    count = lax.axis_size("date")
    return lax.ppermute(block, "date", [(i, (i + step) % count) for i in range(count)])


def split_kernel(kinds, leads, rows, roles, groups, ens_ref, runs_ref, *rest):
    outs, (held, wide, sem) = rest[:-3], rest[-3:]
    block = leads * TILE
    copies = []
    for slot, row in enumerate(rows):
        copy = pltpu.make_async_copy(
            runs_ref.at[pl.ds(row * block * kinds, block * kinds)], held.at[slot], sem.at[slot]
        )
        copy.start()
        copies.append(copy)
    ens = ens_ref[0]
    core, half = ens % 2, ens // 2
    chosen = [
        2 * (1 - half if other_half else half) + (1 - core if other_core else core)
        for other_half, other_core in roles
    ]
    for slot in range(len(rows)):
        group = [i for i, members in enumerate(groups) if rows[slot] in members][0]
        start = groups[group].index(rows[slot]) * block
        copies[slot].wait()
        spread = wide.at[slot % 2]
        spread[...] = held[slot].astype(jnp.float32)
        for role, kind in enumerate(chosen):
            out = outs[group * len(roles) + role]
            for lead in range(0, leads, 2):
                picked = spread[pl.ds(lead * TILE * kinds + kind, 2 * TILE, stride=kinds), :]
                out[start + lead * TILE : start + (lead + 2) * TILE, :] = picked.astype(
                    jnp.bfloat16
                )


def split_kinds(flat, ens, kinds, leads, roles, groups):
    block = leads * TILE
    rows = [row for group in groups for row in group]
    shapes = [
        pltpu.VMEM((len(group) * block, LANES), jnp.bfloat16)
        for group in groups
        for _ in roles
    ]
    outs = pl.pallas_call(
        functools.partial(split_kernel, kinds, leads, rows, roles, groups),
        in_specs=[
            pl.BlockSpec(memory_space=pltpu.SMEM),
            pl.BlockSpec(memory_space=pltpu.HBM),
        ],
        out_specs=[pl.BlockSpec(memory_space=pltpu.VMEM)] * len(shapes),
        scratch_shapes=[
            pltpu.VMEM((len(rows), block * kinds, LANES), jnp.bfloat16),
            pltpu.VMEM((2, block * kinds, LANES), jnp.float32),
            pltpu.SemaphoreType.DMA((len(rows),)),
        ],
        out_shape=shapes,
        cost_estimate=pl.CostEstimate(
            flops=0,
            transcendentals=0,
            bytes_accessed=len(rows) * block * LANES * 2 * (kinds + len(roles)),
        ),
        compiler_params=pltpu.CompilerParams(vmem_limit_bytes=16 * MIB),
    )(ens, pltpu.with_memory_space_constraint(flat, pltpu.HBM))
    return [list(outs[i : i + len(roles)]) for i in range(0, len(shapes), len(roles))]


def smooth_kernel(leads, places, rows, count, extra, weight_ref, *refs):
    sums = refs[:count]
    outs, (done, sem) = refs[-2 - (2 if extra else 1) : -2], refs[-2:]

    def tile(date, lead):
        which, place = places[date]
        start = (place * leads + lead) * TILE
        return sums[which][start : start + TILE, :]

    copies = []
    for slot, row in enumerate(rows):
        weight = [weight_ref[row, k] for k in range(5)]

        def mean(lead):
            value = weight[0] * tile(row - 2, lead)
            for k in range(1, 5):
                value = value + weight[k] * tile(row - 2 + k, lead)
            return value

        before, here = None, mean(0)
        for lead in range(leads):
            after = mean(lead + 1) if lead + 1 < leads else None
            value = here + here
            for beside in (before, after):
                if beside is not None:
                    value = value + beside
            edge = before is None or after is None
            done[slot, lead * TILE : (lead + 1) * TILE, :] = value * (1.0 / 3.0 if edge else 0.25)
            before, here = here, after
        copy = pltpu.make_async_copy(done.at[slot], outs[0].at[row], sem.at[slot])
        copy.start()
        copies.append(copy)
    if extra:
        forecast, kept, given = refs[count : count + 3]
        outs[1][:, 0, :] = forecast[...] - (kept[...] + given[...])
    for copy in copies:
        copy.wait()


def smooth_rows(weights, sums, places, rows, leads, total_rows, extra=(), into=None):
    vmem = pl.BlockSpec(memory_space=pltpu.VMEM)
    smem = pl.BlockSpec(memory_space=pltpu.SMEM)
    hbm = pl.BlockSpec(memory_space=pltpu.HBM)
    operands = [weights, *sums, *extra] + ([] if into is None else [into])
    shapes = [jax.ShapeDtypeStruct((total_rows, leads * TILE, LANES), jnp.float32)]
    if extra:
        shapes.append(jax.ShapeDtypeStruct((WEEKS, 1, LANES), jnp.float32))
    return pl.pallas_call(
        functools.partial(smooth_kernel, leads, places, rows, len(sums), len(extra)),
        in_specs=[smem] + [vmem] * (len(sums) + len(extra)) + ([] if into is None else [hbm]),
        out_specs=[hbm] + ([vmem] if extra else []),
        out_shape=shapes,
        scratch_shapes=[
            pltpu.VMEM((len(rows), leads * TILE, LANES), jnp.float32),
            pltpu.SemaphoreType.DMA((len(rows),)),
        ],
        input_output_aliases={} if into is None else {len(operands) - 1: 0},
        cost_estimate=SMALL,
        compiler_params=pltpu.CompilerParams(vmem_limit_bytes=16 * MIB),
    )(*operands)


def weekly_one_kernel(leads, rows_of, share_ref, table_ref, *refs):
    pairs, out, total = refs[:-2], refs[-2], refs[-1]
    block = leads * TILE
    total[...] = jnp.zeros_like(total)
    for index, rows in enumerate(rows_of):
        first, second = pairs[2 * index], pairs[2 * index + 1]
        for place, row in enumerate(rows):

            @pl.when(share_ref[row] != 0.0)
            def _(first=first, second=second, place=place, row=row):
                span = slice(place * block, (place + 1) * block)
                both = first[span, :].astype(jnp.float32) + second[span, :].astype(jnp.float32)
                total[...] += share_ref[row] * both

    for week in range(WEEKS):
        mean = jnp.zeros((TILE, LANES), jnp.float32)
        for lead in range(leads):
            mean = mean + table_ref[week, lead] * total[lead * TILE : (lead + 1) * TILE, :]
        out[week * TILE : (week + 1) * TILE, :] = mean


def weekly_one(shares, table, leads, rows_of, pairs):
    vmem = pl.BlockSpec(memory_space=pltpu.VMEM)
    smem = pl.BlockSpec(memory_space=pltpu.SMEM)
    return pl.pallas_call(
        functools.partial(weekly_one_kernel, leads, rows_of),
        in_specs=[smem, smem] + [vmem] * len(pairs),
        out_specs=vmem,
        out_shape=jax.ShapeDtypeStruct((WEEKS * TILE, LANES), jnp.float32),
        scratch_shapes=[pltpu.VMEM((leads * TILE, LANES), jnp.float32)],
        cost_estimate=SMALL,
        compiler_params=pltpu.CompilerParams(vmem_limit_bytes=16 * MIB),
    )(shares, table, *pairs)


def date_weights(days, cycle_days):
    columns = []
    for k in (-2, -1, 0, 1, 2):
        if k == 0:
            columns.append(jnp.full(days.shape, 8.0, jnp.float32))
            continue
        other = jnp.roll(days, -k)
        gap = jnp.mod(other - days if k > 0 else days - other, cycle_days)
        columns.append(jnp.maximum(8 - gap, 0).astype(jnp.float32))
    table = jnp.stack(columns, 1)
    return table / jnp.sum(table, 1, keepdims=True)


def lead_smoother(length):
    positions = jnp.arange(length)
    distance = jnp.abs(positions[:, None] - positions[None, :])
    smoother = jnp.where(distance == 0, 2.0, jnp.where(distance == 1, 1.0, 0.0))
    smoother = smoother.astype(jnp.float32)
    return smoother / jnp.sum(smoother, 1, keepdims=True)


def per_device(
    hindcast_runs,
    init_calendar_ordinal,
    prediction_init_position,
    horizon_sevenfold_bin,
    prediction_runs,
):
    highest = lax.Precision.HIGHEST
    _, rows, kinds, leads, cells = hindcast_runs.shape
    slots = lax.axis_size("date")
    dates = rows * slots
    members = lax.axis_size("ens")
    cycle_days = 7 * dates // 2
    block = leads * TILE
    ens = lax.axis_index("ens").astype(jnp.int32)
    date = lax.axis_index("date").astype(jnp.int32)
    ens_operand = ens.reshape(1)

    flat = hindcast_runs.reshape(rows, kinds, leads, TILE, LANES)
    flat = flat.transpose(0, 2, 3, 1, 4).reshape(rows * leads * TILE * kinds, LANES)

    last = 2
    chunks = [
        [0, 1, rows - 2, rows - 1],
        list(range(2, rows - 2 - last)),
        list(range(rows - 2 - last, rows - 2)),
    ]
    split = functools.partial(split_kinds, kinds=kinds, leads=leads)
    for_x = [(True, True), (True, False)]
    for_own = [(False, True), (False, False)]

    def pair_sum(mine, other):
        return ((mine.astype(jnp.float32) + other.astype(jnp.float32)) * SCALE).astype(jnp.float16)

    [sent_0] = split(flat, ens_operand, roles=for_x, groups=chunks[:1])
    got = [core_swap(sent_0[0])]
    flat, *sent_0 = lax.optimization_barrier((flat, *sent_0))
    sent = [sent_0] + split(flat, ens_operand, roles=for_x, groups=chunks[1:])
    got += [core_swap(sent[1][0]), core_swap(sent[2][0])]
    mine, *sent[1] = lax.optimization_barrier((sent[0][1], *sent[1]))
    packed = [pair_sum(mine, got[0])]
    flat, packed[0] = lax.optimization_barrier((flat, packed[0]))
    [[theirs, own]] = split(flat, ens_operand, roles=for_own, groups=[list(range(rows))])
    own_got = core_swap(theirs)
    mine, own = lax.optimization_barrier((sent[1][1], own))
    packed.append(pair_sum(mine, got[1]))
    mine, packed[1] = lax.optimization_barrier((sent[2][1], packed[1]))
    packed.append(pair_sum(mine, got[2]))
    small = (
        init_calendar_ordinal,
        prediction_init_position,
        horizon_sevenfold_bin,
        prediction_runs,
    )
    packed[2], *small = lax.optimization_barrier((packed[2], *small))
    init_calendar_ordinal, prediction_init_position, horizon_sevenfold_bin, prediction_runs = small
    arrived = [chip_swap(block) for block in packed]

    def local_sum(first, count, packed):
        span = slice(first * block, (first + count) * block)
        pair = own[span].astype(jnp.float32) + own_got[span].astype(jnp.float32)
        return pair + packed.astype(jnp.float32) * (1.0 / SCALE)

    low = local_sum(0, 2, arrived[0][: 2 * block])
    high = local_sum(rows - 2, 2, arrived[0][2 * block :])
    below = date_shift(high, 1)
    above = date_shift(low, -1)
    middle = local_sum(chunks[1][0], len(chunks[1]), arrived[1])
    final = local_sum(chunks[2][0], len(chunks[2]), arrived[2])

    weights = date_weights(init_calendar_ordinal, cycle_days)
    own_weights = lax.dynamic_slice_in_dim(weights, date * rows, rows, 0) * (1.0 / members)

    position = prediction_init_position[0]
    row_weights = lax.dynamic_index_in_dim(weights, position, 0, keepdims=False) * (1.0 / members)
    offsets = jnp.mod(date * rows + jnp.arange(rows) - position + 2, dates)
    shares = jnp.sum(
        jnp.where(offsets[:, None] == jnp.arange(5)[None, :], row_weights[None, :], 0.0), 1
    )
    week_table = (
        horizon_sevenfold_bin[None, :] == jnp.arange(WEEKS, dtype=jnp.int32)[:, None]
    ).astype(jnp.float32)
    week_mean = week_table / jnp.sum(week_table, 1, keepdims=True)
    climate_table = jnp.matmul(week_mean, lead_smoother(leads), precision=highest)
    pairs = []
    for (_, mine), other in zip(sent, got):
        pairs += [mine, other]
    weekly = jnp.stack(
        [
            weekly_one(shares, climate_table, leads, chunks, pairs),
            weekly_one(shares, climate_table, leads, [list(range(rows))], [own, own_got]),
        ]
    )
    weekly = weekly.reshape(2, WEEKS, slots, LANES).transpose(2, 0, 1, 3)
    weekly, low, high = lax.optimization_barrier((weekly, low, high))
    weekly = lax.all_to_all(weekly, "date", split_axis=0, concat_axis=0, tiled=True)
    weekly = jnp.sum(weekly, 0, keepdims=True)
    weekly_given = chip_swap(weekly[0, 0])
    centroid = jnp.sum(prediction_runs[:, 0].astype(jnp.float32), 0) * (
        1.0 / prediction_runs.shape[0]
    )
    forecast = jnp.einsum("wl,lp->wp", week_mean, centroid, precision=highest)

    places = {-2: (0, 0), -1: (0, 1), 0: (1, 0), 1: (1, 1)}
    places |= {row: (2, i) for i, row in enumerate(chunks[1])}
    places |= {rows - 2: (3, 0), rows - 1: (3, 1), rows: (4, 0), rows + 1: (4, 1)}
    places |= {row: (5, i) for i, row in enumerate(chunks[2])}
    ready = chunks[1][-1] - 1
    [smoothed] = smooth_rows(
        own_weights, [below, low, middle], places, list(range(ready)), leads, rows
    )
    smoothed, anomalies = smooth_rows(
        own_weights,
        [below, low, middle, high, above, final],
        places,
        list(range(ready, rows)),
        leads,
        rows,
        (forecast, weekly[0, 1], weekly_given),
        smoothed,
    )
    return smoothed.reshape(rows, 1, leads, cells), anomalies


def solution(mesh):
    return jax.shard_map(
        per_device,
        mesh=mesh,
        in_specs=(
            P("ens", "date", None, None, "pix"),
            P(),
            P(),
            P(),
            P(None, "ens", None, ("pix", "date")),
        ),
        out_specs=(P("date", "ens", None, "pix"), P(None, "ens", ("pix", "date"))),
        check_vma=False,
    )
```

```python
import functools

import jax
import jax.numpy as jnp
from jax import lax
from jax.experimental import pallas as pl
from jax.experimental.pallas import tpu as pltpu
from jax.sharding import PartitionSpec as P

WEEKS = 7
LANES = 128
TILE = 8
SCALE = 512.0
MIB = 1024 * 1024
SMEM = pl.BlockSpec(memory_space=pltpu.SMEM)
VMEM = pl.BlockSpec(memory_space=pltpu.VMEM)
HBM = pl.BlockSpec(memory_space=pltpu.HBM)


def estimate(num_bytes):
    return pl.CostEstimate(flops=1, transcendentals=0, bytes_accessed=num_bytes)


def core_swap(block):
    return lax.ppermute(block, "ens", [(0, 1), (1, 0), (2, 3), (3, 2)])


def chip_swap(block):
    return lax.ppermute(block, "ens", [(0, 2), (1, 3), (2, 0), (3, 1)])


def date_shift(block, step):
    count = lax.axis_size("date")
    return lax.ppermute(block, "date", [(i, (i + step) % count) for i in range(count)])


def split_kernel(kinds, leads, rows, wanted, ens_ref, runs_ref, *rest):
    outs, (held, wide, sem) = rest[:-3], rest[-3:]
    block = leads * TILE
    copies = []
    for slot, row in enumerate(rows):
        copy = pltpu.make_async_copy(
            runs_ref.at[pl.ds(row * block * kinds, block * kinds)], held.at[slot], sem.at[slot]
        )
        copy.start()
        copies.append(copy)
    ens = ens_ref[0]
    core, half = ens % 2, ens // 2
    for slot, row in enumerate(rows):
        copies[slot].wait()
        spread = wide.at[slot % 2]
        spread[...] = held[slot].astype(jnp.float32)
        for out, (members, other_half, other_core) in zip(outs, wanted):
            if row not in members:
                continue
            kind = 2 * (1 - half if other_half else half) + (1 - core if other_core else core)
            start = members.index(row) * block
            for lead in range(0, leads, 2):
                picked = spread[pl.ds(lead * TILE * kinds + kind, 2 * TILE, stride=kinds), :]
                out[start + lead * TILE : start + (lead + 2) * TILE, :] = picked.astype(
                    jnp.bfloat16
                )


def split_kinds(flat, ens, kinds, leads, rows, wanted):
    block = leads * TILE
    shapes = [pltpu.VMEM((len(members) * block, LANES), jnp.bfloat16) for members, _, _ in wanted]
    outs = pl.pallas_call(
        functools.partial(split_kernel, kinds, leads, rows, wanted),
        in_specs=[SMEM, HBM],
        out_specs=[VMEM] * len(shapes),
        scratch_shapes=[
            pltpu.VMEM((len(rows), block * kinds, LANES), jnp.bfloat16),
            pltpu.VMEM((2, block * kinds, LANES), jnp.float32),
            pltpu.SemaphoreType.DMA((len(rows),)),
        ],
        out_shape=shapes,
        cost_estimate=estimate(len(rows) * block * LANES * 2 * kinds),
        compiler_params=pltpu.CompilerParams(vmem_limit_bytes=10 * MIB),
    )(ens, pltpu.with_memory_space_constraint(flat, pltpu.HBM))
    return list(outs)


def wrapped(index, count):
    index = jnp.where(index < 0, index + count, index)
    return jnp.where(index >= count, index - count, index)


def neighbour_weights(days_ref, date, cycle_days):
    count = days_ref.shape[0]
    weights = []
    for k in range(-2, 3):
        other = days_ref[wrapped(date + k, count)]
        gap = other - days_ref[date] if k >= 0 else days_ref[date] - other
        gap = jnp.where(gap < 0, gap + cycle_days, gap)
        weights.append(jnp.maximum(8 - gap, 0).astype(jnp.float32))
    total = weights[0] + weights[1] + weights[2] + weights[3] + weights[4]
    return weights, 1.0 / jnp.full((TILE, LANES), total, jnp.float32)


def smoothed_leads(leads, value):
    before, here = None, value(0)
    for lead in range(leads):
        after = value(lead + 1) if lead + 1 < leads else None
        total = here + here
        for beside in (before, after):
            if beside is not None:
                total = total + beside
        yield lead, total * (1.0 / 3.0 if before is None or after is None else 0.25)
        before, here = here, after


def smooth_kernel(leads, places, rows, members, cycle_days, date_ref, days_ref, *refs):
    sums, (forecast, kept, given, out_hbm, anomalies, done, sem) = refs[:-7], refs[-7:]

    def tile(row, lead):
        which, place = places[row]
        start = (place * leads + lead) * TILE
        return sums[which][start : start + TILE, :]

    copies = []
    for row in range(rows):
        weights, inverse = neighbour_weights(days_ref, date_ref[0] * rows + row, cycle_days)
        inverse = inverse * (1.0 / members)

        def mean(lead):
            value = weights[0] * tile(row - 2, lead)
            for k in range(1, 5):
                value = value + weights[k] * tile(row - 2 + k, lead)
            return value * inverse

        for lead, value in smoothed_leads(leads, mean):
            done[row, lead * TILE : (lead + 1) * TILE, :] = value
        copy = pltpu.make_async_copy(done.at[row], out_hbm.at[row], sem.at[row])
        copy.start()
        copies.append(copy)
    anomalies[:, 0, :] = forecast[...] - (kept[WEEKS:, :] + given[...])
    for copy in copies:
        copy.wait()


def smooth_rows(date, days, sums, extra, places, rows, leads, members, cycle_days):
    return pl.pallas_call(
        functools.partial(smooth_kernel, leads, places, rows, members, cycle_days),
        in_specs=[SMEM, SMEM] + [VMEM] * (len(sums) + len(extra)),
        out_specs=[HBM, VMEM],
        out_shape=[
            jax.ShapeDtypeStruct((rows, leads * TILE, LANES), jnp.float32),
            jax.ShapeDtypeStruct((WEEKS, 1, LANES), jnp.float32),
        ],
        scratch_shapes=[
            pltpu.VMEM((rows, leads * TILE, LANES), jnp.float32),
            pltpu.SemaphoreType.DMA((rows,)),
        ],
        cost_estimate=estimate(1),
        compiler_params=pltpu.CompilerParams(vmem_limit_bytes=10 * MIB),
    )(date, days, *sums, *extra)


def weekly_kernel(
    kinds, leads, rows, members, cycle_days, ens_ref, date_ref, days_ref, position_ref, bins_ref, *refs
):
    forecast_ref, runs_ref, *outs, climate, held, sem, weekly, means, counts = refs
    block = leads * TILE * kinds
    group = TILE * kinds
    position = position_ref[0]
    dates = days_ref.shape[0]
    weights, inverse = neighbour_weights(days_ref, position, cycle_days)
    inverse = inverse * (1.0 / members)
    for week in range(WEEKS):
        counts[week] = 0
    for lead in range(leads):
        counts[bins_ref[lead]] += 1

    row_of = [wrapped(position + k - 2, dates) - date_ref[0] * rows for k in range(5)]
    here = [(row >= 0) & (row < rows) for row in row_of]

    def copy_of(k):
        start = pl.multiple_of(row_of[k] * block, 16)
        return pltpu.make_async_copy(runs_ref.at[pl.ds(start, block)], held.at[k], sem.at[k])

    for k in range(5):

        @pl.when(here[k])
        def _():
            copy_of(k).start()

    total = forecast_ref[0].astype(jnp.float32)
    for run in range(1, forecast_ref.shape[0]):
        total = total + forecast_ref[run].astype(jnp.float32)
    climate[:leads, :] = total
    means[...] = jnp.zeros_like(means)
    for lead in range(leads):
        means[pl.ds(bins_ref[lead], 1), :] += climate[lead : lead + 1, :]
    for week in range(WEEKS):
        count = jnp.full((1, LANES), (counts[week] * forecast_ref.shape[0]).astype(jnp.float32))
        outs[1][week : week + 1, :] = means[week : week + 1, :] / count

    climate[...] = jnp.zeros_like(climate)
    weekly[...] = jnp.zeros_like(weekly)
    for k in range(5):

        @pl.when(here[k])
        def _():
            copy_of(k).wait()
            climate[...] += weights[k] * held[k].astype(jnp.float32)

    @pl.when(here[0] | here[1] | here[2] | here[3] | here[4])
    def _():
        def part(lead):
            return climate[lead * group : (lead + 1) * group, :]

        for lead, value in smoothed_leads(leads, part):
            span = pl.ds(pl.multiple_of(bins_ref[lead] * group, group), group)
            weekly[span, :] += value

    core, half = ens_ref[0] % 2, ens_ref[0] // 2
    order = [(1 - half, 1 - core), (half, 1 - core), (1 - half, core), (half, core)]
    for week in range(WEEKS):
        scale = inverse / jnp.full((TILE, LANES), counts[week].astype(jnp.float32))
        for role, (of_half, of_core) in enumerate(order):
            kind = 2 * of_half + of_core
            mean = weekly[pl.ds(week * group + kind, TILE, stride=kinds), :] * scale
            for slot in range(TILE):
                outs[0][slot, role * WEEKS + week, :] = mean[slot]


def weekly_means(ens, date, days, position, bins, forecast, flat, kinds, leads, rows, members, cycle_days):
    return pl.pallas_call(
        functools.partial(weekly_kernel, kinds, leads, rows, members, cycle_days),
        in_specs=[SMEM] * 5 + [VMEM, HBM],
        out_specs=[VMEM, VMEM],
        out_shape=[
            jax.ShapeDtypeStruct((TILE, kinds * WEEKS, LANES), jnp.float32),
            jax.ShapeDtypeStruct((WEEKS, LANES), jnp.float32),
        ],
        scratch_shapes=[
            pltpu.VMEM((leads * TILE * kinds, LANES), jnp.float32),
            pltpu.VMEM((5, leads * TILE * kinds, LANES), jnp.bfloat16),
            pltpu.SemaphoreType.DMA((5,)),
            pltpu.VMEM((WEEKS * TILE * kinds, LANES), jnp.float32),
            pltpu.VMEM((TILE, LANES), jnp.float32),
            pltpu.SMEM((WEEKS,), jnp.int32),
        ],
        cost_estimate=estimate(1),
        compiler_params=pltpu.CompilerParams(vmem_limit_bytes=10 * MIB),
    )(ens, date, days, position, bins, forecast, pltpu.with_memory_space_constraint(flat, pltpu.HBM))


def per_device(
    hindcast_runs,
    init_calendar_ordinal,
    prediction_init_position,
    horizon_sevenfold_bin,
    prediction_runs,
):
    _, rows, kinds, leads, cells = hindcast_runs.shape
    dates = rows * lax.axis_size("date")
    members = lax.axis_size("ens")
    cycle_days = 7 * dates // 2
    block = leads * TILE
    ens = lax.axis_index("ens").astype(jnp.int32).reshape(1)
    date = lax.axis_index("date").astype(jnp.int32).reshape(1)

    flat = hindcast_runs.reshape(rows, kinds, leads, TILE, LANES)
    flat = flat.transpose(0, 2, 3, 1, 4).reshape(rows * leads * TILE * kinds, LANES)

    chunks = [[0, 1, 2, rows - 2, rows - 1], list(range(3, rows - 2))]
    split = functools.partial(split_kinds, kinds=kinds, leads=leads)
    edge, inner, every = chunks[0], chunks[1], list(range(rows))

    def pair_sum(mine, other):
        return ((mine.astype(jnp.float32) + other.astype(jnp.float32)) * SCALE).astype(jnp.float16)

    theirs_0, mine_0 = split(flat, ens, rows=edge, wanted=[(edge, True, True), (edge, True, False)])
    got_0 = core_swap(theirs_0)
    flat, mine_0 = lax.optimization_barrier((flat, mine_0))
    theirs_1, mine_1, theirs, own = split(
        flat,
        ens,
        rows=inner + edge,
        wanted=[
            (inner, True, True),
            (inner, True, False),
            (every, False, True),
            (every, False, False),
        ],
    )
    got_1 = core_swap(theirs_1)
    own_got = core_swap(theirs)
    mine_0, mine_1 = lax.optimization_barrier((mine_0, mine_1))
    packed_0 = pair_sum(mine_0, got_0)
    mine_1, packed_0 = lax.optimization_barrier((mine_1, packed_0))
    packed_1 = pair_sum(mine_1, got_1)
    flat, packed_1 = lax.optimization_barrier((flat, packed_1))
    arrived_0 = chip_swap(packed_0)
    arrived_1 = chip_swap(packed_1)

    def local_sum(first, count, packed):
        span = slice(first * block, (first + count) * block)
        pair = own[span].astype(jnp.float32) + own_got[span].astype(jnp.float32)
        return pair + packed.astype(jnp.float32) * (1.0 / SCALE)

    low = local_sum(0, 2, arrived_0[: 2 * block])
    high = local_sum(rows - 2, 2, arrived_0[-2 * block :])
    below = date_shift(high, 1)
    above = date_shift(low, -1)
    third = local_sum(2, 1, arrived_0[2 * block : 3 * block])
    middle = local_sum(inner[0], len(inner), arrived_1)

    weekly, forecast = weekly_means(
        ens,
        date,
        init_calendar_ordinal,
        prediction_init_position,
        horizon_sevenfold_bin,
        prediction_runs[:, 0],
        flat,
        kinds,
        leads,
        rows,
        members,
        cycle_days,
    )
    weekly = jnp.sum(lax.all_to_all(weekly, "date", split_axis=0, concat_axis=0, tiled=True), 0)
    weekly = weekly[2 * WEEKS :] + core_swap(weekly[: 2 * WEEKS])
    given = chip_swap(weekly[:WEEKS])

    places = {-2: (0, 0), -1: (0, 1), 0: (1, 0), 1: (1, 1)}
    places |= {2: (5, 0)} | {row: (2, i) for i, row in enumerate(inner)}
    places |= {rows - 2: (3, 0), rows - 1: (3, 1), rows: (4, 0), rows + 1: (4, 1)}
    smoothed, anomalies = smooth_rows(
        date,
        init_calendar_ordinal,
        [below, low, middle, high, above, third],
        [forecast, weekly, given],
        places,
        rows,
        leads,
        members,
        cycle_days,
    )
    return smoothed.reshape(rows, 1, leads, cells), anomalies


def solution(mesh):
    return jax.shard_map(
        per_device,
        mesh=mesh,
        in_specs=(
            P("ens", "date", None, None, "pix"),
            P(),
            P(),
            P(),
            P(None, "ens", None, ("pix", "date")),
        ),
        out_specs=(P("date", "ens", None, "pix"), P(None, "ens", ("pix", "date"))),
        check_vma=False,
    )
```

```python
import functools

import jax
import jax.numpy as jnp
from jax import lax
from jax.experimental import pallas as pl
from jax.experimental.pallas import tpu as pltpu
from jax.sharding import PartitionSpec as P

WEEKS = 7
LANES = 128
TILE = 8
SCALE = 512.0
MIB = 1024 * 1024
SMEM = pl.BlockSpec(memory_space=pltpu.SMEM)
VMEM = pl.BlockSpec(memory_space=pltpu.VMEM)
HBM = pl.BlockSpec(memory_space=pltpu.HBM)


def estimate(num_bytes):
    return pl.CostEstimate(flops=1, transcendentals=0, bytes_accessed=num_bytes)


def core_swap(block):
    return lax.ppermute(block, "ens", [(0, 1), (1, 0), (2, 3), (3, 2)])


def chip_swap(block):
    return lax.ppermute(block, "ens", [(0, 2), (1, 3), (2, 0), (3, 1)])


def date_shift(block, step):
    count = lax.axis_size("date")
    return lax.ppermute(block, "date", [(i, (i + step) % count) for i in range(count)])


def split_rows(kinds, leads, rows, wanted, ens_ref, copies, held, wide, outs):
    block = leads * TILE
    core, half = ens_ref[0] % 2, ens_ref[0] // 2
    for slot, row in enumerate(rows):
        copies[slot].wait()
        spread = wide.at[slot % 2]
        spread[...] = held[slot].astype(jnp.float32)
        for out, (members, other_half, other_core) in zip(outs, wanted):
            if row not in members:
                continue
            kind = 2 * (1 - half if other_half else half) + (1 - core if other_core else core)
            start = members.index(row) * block
            for lead in range(0, leads, 2):
                picked = spread[pl.ds(lead * TILE * kinds + kind, 2 * TILE, stride=kinds), :]
                out[start + lead * TILE : start + (lead + 2) * TILE, :] = picked.astype(
                    jnp.bfloat16
                )


def start_rows(rows, block, runs_ref, held, sem):
    copies = []
    for slot, row in enumerate(rows):
        copy = pltpu.make_async_copy(
            runs_ref.at[pl.ds(row * block, block)], held.at[slot], sem.at[slot]
        )
        copy.start()
        copies.append(copy)
    return copies


def split_kernel(kinds, leads, rows, wanted, ens_ref, runs_ref, *rest):
    outs, (held, wide, sem) = rest[:-3], rest[-3:]
    copies = start_rows(rows, leads * TILE * kinds, runs_ref, held, sem)
    split_rows(kinds, leads, rows, wanted, ens_ref, copies, held, wide, outs)


def split_scratch(rows, block):
    return [
        pltpu.VMEM((len(rows), block, LANES), jnp.bfloat16),
        pltpu.VMEM((2, block, LANES), jnp.float32),
        pltpu.SemaphoreType.DMA((len(rows),)),
    ]


def split_kinds(flat, ens, kinds, leads, rows, wanted):
    block = leads * TILE
    shapes = [pltpu.VMEM((len(members) * block, LANES), jnp.bfloat16) for members, _, _ in wanted]
    outs = pl.pallas_call(
        functools.partial(split_kernel, kinds, leads, rows, wanted),
        in_specs=[SMEM, HBM],
        out_specs=[VMEM] * len(shapes),
        scratch_shapes=split_scratch(rows, block * kinds),
        out_shape=shapes,
        cost_estimate=estimate(len(rows) * block * LANES * 2 * kinds),
        compiler_params=pltpu.CompilerParams(vmem_limit_bytes=10 * MIB),
    )(ens, pltpu.with_memory_space_constraint(flat, pltpu.HBM))
    return list(outs)


def wrapped(index, count):
    index = jnp.where(index < 0, index + count, index)
    return jnp.where(index >= count, index - count, index)


def neighbour_weights(days_ref, date, cycle_days):
    count = days_ref.shape[0]
    weights = []
    for k in range(-2, 3):
        other = days_ref[wrapped(date + k, count)]
        gap = other - days_ref[date] if k >= 0 else days_ref[date] - other
        gap = jnp.where(gap < 0, gap + cycle_days, gap)
        weights.append(jnp.maximum(8 - gap, 0).astype(jnp.float32))
    total = weights[0] + weights[1] + weights[2] + weights[3] + weights[4]
    return weights, 1.0 / jnp.full((TILE, LANES), total, jnp.float32)


def smoothed_leads(leads, value):
    before, here = None, value(0)
    for lead in range(leads):
        after = value(lead + 1) if lead + 1 < leads else None
        total = here + here
        for beside in (before, after):
            if beside is not None:
                total = total + beside
        yield lead, total * (1.0 / 3.0 if before is None or after is None else 0.25)
        before, here = here, after


def smooth_kernel(leads, places, rows, total_rows, members, cycle_days, count, date_ref, days_ref, *refs):
    sums, (out_hbm, done, sem) = refs[:count], refs[-3:]

    def tile(row, lead):
        which, place = places[row]
        start = (place * leads + lead) * TILE
        return sums[which][start : start + TILE, :]

    copies = []
    for slot, row in enumerate(rows):
        weights, inverse = neighbour_weights(days_ref, date_ref[0] * total_rows + row, cycle_days)
        inverse = inverse * (1.0 / members)

        def mean(lead):
            value = weights[0] * tile(row - 2, lead)
            for k in range(1, 5):
                value = value + weights[k] * tile(row - 2 + k, lead)
            return value * inverse

        for lead, value in smoothed_leads(leads, mean):
            done[slot, lead * TILE : (lead + 1) * TILE, :] = value
        copy = pltpu.make_async_copy(done.at[slot], out_hbm.at[row], sem.at[slot])
        copy.start()
        copies.append(copy)
    for copy in copies:
        copy.wait()


def smooth_rows(date, days, arrays, rows, total_rows, leads, members, cycle_days, cost, into=None):
    places = {row: (i, j) for i, (_, held) in enumerate(arrays) for j, row in enumerate(held)}
    sums = [array for array, _ in arrays]
    operands = [date, days, *sums] + ([] if into is None else [into])
    return pl.pallas_call(
        functools.partial(
            smooth_kernel, leads, places, rows, total_rows, members, cycle_days, len(sums)
        ),
        in_specs=[SMEM, SMEM] + [VMEM] * len(sums) + ([] if into is None else [HBM]),
        out_specs=HBM,
        out_shape=jax.ShapeDtypeStruct((total_rows, leads * TILE, LANES), jnp.float32),
        scratch_shapes=[
            pltpu.VMEM((len(rows), leads * TILE, LANES), jnp.float32),
            pltpu.SemaphoreType.DMA((len(rows),)),
        ],
        input_output_aliases={} if into is None else {len(operands) - 1: 0},
        cost_estimate=estimate(cost),
        compiler_params=pltpu.CompilerParams(vmem_limit_bytes=8 * MIB),
    )(*operands)


def anomaly_kernel(forecast, kept, given, out):
    out[:, 0, :] = forecast[...] - (kept[...] + given[...])


def weekly_anomalies(forecast, kept, given):
    return pl.pallas_call(
        anomaly_kernel,
        in_specs=[VMEM] * 3,
        out_specs=VMEM,
        out_shape=jax.ShapeDtypeStruct((WEEKS, 1, LANES), jnp.float32),
        cost_estimate=estimate(1),
        compiler_params=pltpu.CompilerParams(vmem_limit_bytes=MIB),
    )(forecast, kept, given)


def count_weeks(leads, bins_ref, counts):
    for week in range(WEEKS):
        counts[week] = 0
    for lead in range(leads):
        counts[bins_ref[lead]] += 1


def weekly_kernel(
    kinds, leads, rows, members, cycle_days, ens_ref, date_ref, days_ref, position_ref, bins_ref, *refs
):
    runs_ref, give, keep, climate, near, sem, weekly, counts = refs
    group = TILE * kinds
    block = leads * group
    position = position_ref[0]
    dates = days_ref.shape[0]
    row_of = [wrapped(position + k - 2, dates) - date_ref[0] * rows for k in range(5)]
    here = [(row >= 0) & (row < rows) for row in row_of]

    def copy_of(k):
        start = pl.multiple_of(row_of[k] * block, 16)
        return pltpu.make_async_copy(runs_ref.at[pl.ds(start, block)], near.at[k], sem.at[k])

    for k in range(5):

        @pl.when(here[k])
        def _():
            copy_of(k).start()

    weights, inverse = neighbour_weights(days_ref, position, cycle_days)
    inverse = inverse * (1.0 / members)
    count_weeks(leads, bins_ref, counts)
    weekly[...] = jnp.zeros_like(weekly)

    @pl.when(here[0] | here[1] | here[2] | here[3] | here[4])
    def _():
        climate[...] = jnp.zeros_like(climate)
        for k in range(5):

            @pl.when(here[k])
            def _():
                copy_of(k).wait()
                climate[...] += weights[k] * near[k].astype(jnp.float32)

        def part(lead):
            return climate[lead * group : (lead + 1) * group, :]

        for lead, value in smoothed_leads(leads, part):
            span = pl.ds(pl.multiple_of(bins_ref[lead] * group, group), group)
            weekly[span, :] += value

    core, half = ens_ref[0] % 2, ens_ref[0] // 2
    for week in range(WEEKS):
        scale = inverse / jnp.full((TILE, LANES), counts[week].astype(jnp.float32))
        for role, of_half in enumerate((1 - half, half)):
            for out, of_core in ((give, 1 - core), (keep, core)):
                kind = 2 * of_half + of_core
                mean = weekly[pl.ds(week * group + kind, TILE, stride=kinds), :] * scale
                for slot in range(TILE):
                    out[role * TILE + slot, week, :] = mean[slot]


def weekly_shares(ens, date, days, position, bins, flat, kinds, leads, rows, members, cycle_days):
    block = leads * TILE * kinds
    shape = pltpu.VMEM((2 * TILE, WEEKS, LANES), jnp.float32)
    return pl.pallas_call(
        functools.partial(weekly_kernel, kinds, leads, rows, members, cycle_days),
        in_specs=[SMEM] * 5 + [HBM],
        out_specs=[VMEM] * 2,
        out_shape=[shape] * 2,
        scratch_shapes=[
            pltpu.VMEM((block, LANES), jnp.float32),
            pltpu.VMEM((5, block, LANES), jnp.bfloat16),
            pltpu.SemaphoreType.DMA((5,)),
            pltpu.VMEM((WEEKS * TILE * kinds, LANES), jnp.float32),
            pltpu.SMEM((WEEKS,), jnp.int32),
        ],
        cost_estimate=estimate(1),
        compiler_params=pltpu.CompilerParams(vmem_limit_bytes=8 * MIB),
    )(ens, date, days, position, bins, pltpu.with_memory_space_constraint(flat, pltpu.HBM))


def forecast_kernel(leads, bins_ref, forecast_ref, out, total, means, counts):
    count_weeks(leads, bins_ref, counts)
    runs = forecast_ref.shape[0]
    value = forecast_ref[0].astype(jnp.float32)
    for run in range(1, runs):
        value = value + forecast_ref[run].astype(jnp.float32)
    total[...] = value
    means[...] = jnp.zeros_like(means)
    for lead in range(leads):
        means[pl.ds(bins_ref[lead], 1), :] += total[lead : lead + 1, :]
    for week in range(WEEKS):
        count = jnp.full((1, LANES), (counts[week] * runs).astype(jnp.float32))
        out[week : week + 1, :] = means[week : week + 1, :] / count


def forecast_weeks(bins, forecast, leads):
    return pl.pallas_call(
        functools.partial(forecast_kernel, leads),
        in_specs=[SMEM, VMEM],
        out_specs=VMEM,
        out_shape=jax.ShapeDtypeStruct((WEEKS, LANES), jnp.float32),
        scratch_shapes=[
            pltpu.VMEM((leads, LANES), jnp.float32),
            pltpu.VMEM((TILE, LANES), jnp.float32),
            pltpu.SMEM((WEEKS,), jnp.int32),
        ],
        cost_estimate=estimate(1),
        compiler_params=pltpu.CompilerParams(vmem_limit_bytes=4 * MIB),
    )(bins, forecast)


def date_bits():
    slot = lax.axis_index("date").astype(jnp.uint32)
    steps = [1 << bit for bit in range(lax.axis_size("date").bit_length() - 1)][::-1]
    return [number for step in steps for number in ((slot // step) & 1, ((slot // step) & 1) ^ 1)]


def weeks_over_dates(total, bits):
    slots = lax.axis_size("date")
    step = slots // 2
    for mine, other in zip(bits[::2], bits[1::2]):
        halves = total.reshape(2, step, *total.shape[1:])
        give = lax.dynamic_index_in_dim(halves, other, 0, keepdims=False)
        keep = lax.dynamic_index_in_dim(halves, mine, 0, keepdims=False)
        got = lax.ppermute(give, "date", [(i, i ^ step) for i in range(slots)])
        total = keep + got
        step //= 2
    return keep[0], got[0]


def per_device(
    hindcast_runs,
    init_calendar_ordinal,
    prediction_init_position,
    horizon_sevenfold_bin,
    prediction_runs,
):
    _, rows, kinds, leads, cells = hindcast_runs.shape
    dates = rows * lax.axis_size("date")
    members = lax.axis_size("ens")
    cycle_days = 7 * dates // 2
    block = leads * TILE
    ens = lax.axis_index("ens").astype(jnp.int32).reshape(1)
    date = lax.axis_index("date").astype(jnp.int32).reshape(1)

    numbers = date_bits()

    flat = hindcast_runs.reshape(rows, kinds, leads, TILE, LANES)
    flat = flat.transpose(0, 2, 3, 1, 4).reshape(rows * leads * TILE * kinds, LANES)
    flat, ens, date, *numbers = lax.optimization_barrier((flat, ens, date, *numbers))

    first = [0, 1, rows - 2, rows - 1]
    second = list(range(2, rows - 2))
    split = functools.partial(split_kinds, kinds=kinds, leads=leads)

    def for_x(flat, members):
        return split(flat, ens, rows=members, wanted=[(members, True, True), (members, True, False)])

    def pair_sum(mine, other):
        return ((mine.astype(jnp.float32) + other.astype(jnp.float32)) * SCALE).astype(jnp.float16)

    theirs_0, mine_0 = for_x(flat, first)
    got_0 = core_swap(theirs_0)
    flat, mine_0 = lax.optimization_barrier((flat, mine_0))
    theirs_1, mine_1 = for_x(flat, second)
    got_1 = core_swap(theirs_1)
    flat, mine_1 = lax.optimization_barrier((flat, mine_1))
    weeks_give, weeks_keep = weekly_shares(
        ens,
        date,
        init_calendar_ordinal,
        prediction_init_position,
        horizon_sevenfold_bin,
        flat,
        kinds,
        leads,
        rows,
        members,
        cycle_days,
    )
    mine_0, weeks_keep = lax.optimization_barrier((mine_0, weeks_keep))
    packed_0 = pair_sum(mine_0, got_0)
    packed_0, weeks_give = lax.optimization_barrier((packed_0, weeks_give))
    weeks_got = core_swap(weeks_give)
    arrived_0 = chip_swap(packed_0)
    flat, packed_0, mine_1 = lax.optimization_barrier((flat, packed_0, mine_1))
    packed_1 = pair_sum(mine_1, got_1)
    arrived_1 = chip_swap(packed_1)
    parts = [first, second]
    own = split(
        flat,
        ens,
        rows=first + second,
        wanted=[(part, False, other) for part in parts for other in (True, False)],
    )
    others = [core_swap(theirs) for theirs in own[::2]]

    weeks = weeks_keep + weeks_got
    weeks = weeks[TILE:] + chip_swap(weeks[:TILE])
    def local_sum(own, other, own_place, packed, place, count):
        own_span = slice(own_place * block, (own_place + count) * block)
        pair = own[own_span].astype(jnp.float32) + other[own_span].astype(jnp.float32)
        span = slice(place * block, (place + count) * block)
        return pair + packed[span].astype(jnp.float32) * (1.0 / SCALE)

    low = local_sum(own[1], others[0], 0, arrived_0, 0, 2)
    high = local_sum(own[1], others[0], 2, arrived_0, 2, 2)
    weeks, low, high = lax.optimization_barrier((weeks, low, high))
    kept, given = weeks_over_dates(weeks, numbers)
    below = date_shift(high, 1)
    above = date_shift(low, -1)
    middle = local_sum(own[3], others[1], 0, arrived_1, 0, len(second))

    forecast = forecast_weeks(horizon_sevenfold_bin, prediction_runs[:, 0], leads)

    arrays = [
        (below, [-2, -1]),
        (low, [0, 1]),
        (middle, second),
        (high, [rows - 2, rows - 1]),
        (above, [rows, rows + 1]),
    ]
    smooth = functools.partial(
        smooth_rows,
        date,
        init_calendar_ordinal,
        total_rows=rows,
        leads=leads,
        members=members,
        cycle_days=cycle_days,
    )
    smoothed = smooth(arrays[1:-1], list(range(2, rows - 2)), cost=10 * MIB)
    smoothed = smooth(arrays, [0, 1, rows - 2, rows - 1], cost=1, into=smoothed)
    return smoothed.reshape(rows, 1, leads, cells), weekly_anomalies(forecast, kept, given)


def solution(mesh):
    return jax.shard_map(
        per_device,
        mesh=mesh,
        in_specs=(
            P("ens", "date", None, None, "pix"),
            P(),
            P(),
            P(),
            P(None, "ens", None, ("pix", "date")),
        ),
        out_specs=(P("date", "ens", None, "pix"), P(None, "ens", ("pix", "date"))),
        check_vma=False,
    )
```

```python
import functools

import jax
import jax.numpy as jnp
from jax import lax
from jax.experimental import pallas as pl
from jax.experimental.pallas import tpu as pltpu
from jax.sharding import PartitionSpec as P

WEEKS = 7
LANES = 128
TILE = 8
SCALE = 512.0
MIB = 1024 * 1024
SMEM = pl.BlockSpec(memory_space=pltpu.SMEM)
VMEM = pl.BlockSpec(memory_space=pltpu.VMEM)
HBM = pl.BlockSpec(memory_space=pltpu.HBM)


def estimate(num_bytes):
    return pl.CostEstimate(flops=1, transcendentals=0, bytes_accessed=num_bytes)


def core_swap(block):
    return lax.ppermute(block, "ens", [(0, 1), (1, 0), (2, 3), (3, 2)])


def chip_swap(block):
    return lax.ppermute(block, "ens", [(0, 2), (1, 3), (2, 0), (3, 1)])


def date_shift(block, step):
    count = lax.axis_size("date")
    return lax.ppermute(block, "date", [(i, (i + step) % count) for i in range(count)])


def split_rows(kinds, leads, rows, wanted, ens_ref, copies, held, wide, outs):
    block = leads * TILE
    core, half = ens_ref[0] % 2, ens_ref[0] // 2
    for slot, row in enumerate(rows):
        copies[slot].wait()
        spread = wide.at[slot % 2]
        spread[...] = held[slot].astype(jnp.float32)
        for out, (members, other_half, other_core) in zip(outs, wanted):
            if row not in members:
                continue
            kind = 2 * (1 - half if other_half else half) + (1 - core if other_core else core)
            start = members.index(row) * block
            for lead in range(0, leads, 2):
                picked = spread[pl.ds(lead * TILE * kinds + kind, 2 * TILE, stride=kinds), :]
                out[start + lead * TILE : start + (lead + 2) * TILE, :] = picked.astype(
                    jnp.bfloat16
                )


def start_rows(rows, block, runs_ref, held, sem):
    copies = []
    for slot, row in enumerate(rows):
        copy = pltpu.make_async_copy(
            runs_ref.at[pl.ds(row * block, block)], held.at[slot], sem.at[slot]
        )
        copy.start()
        copies.append(copy)
    return copies


def split_kernel(kinds, leads, rows, wanted, ens_ref, runs_ref, *rest):
    outs, (held, wide, sem) = rest[:-3], rest[-3:]
    copies = start_rows(rows, leads * TILE * kinds, runs_ref, held, sem)
    split_rows(kinds, leads, rows, wanted, ens_ref, copies, held, wide, outs)


def split_scratch(rows, block):
    return [
        pltpu.VMEM((len(rows), block, LANES), jnp.bfloat16),
        pltpu.VMEM((2, block, LANES), jnp.float32),
        pltpu.SemaphoreType.DMA((len(rows),)),
    ]


def split_kinds(flat, ens, kinds, leads, rows, wanted):
    block = leads * TILE
    shapes = [pltpu.VMEM((len(members) * block, LANES), jnp.bfloat16) for members, _, _ in wanted]
    outs = pl.pallas_call(
        functools.partial(split_kernel, kinds, leads, rows, wanted),
        in_specs=[SMEM, HBM],
        out_specs=[VMEM] * len(shapes),
        scratch_shapes=split_scratch(rows, block * kinds),
        out_shape=shapes,
        cost_estimate=estimate(len(rows) * block * LANES * 2 * kinds),
        compiler_params=pltpu.CompilerParams(vmem_limit_bytes=10 * MIB),
    )(ens, pltpu.with_memory_space_constraint(flat, pltpu.HBM))
    return list(outs)


def wrapped(index, count):
    index = jnp.where(index < 0, index + count, index)
    return jnp.where(index >= count, index - count, index)


def neighbour_weights(days_ref, date, cycle_days):
    count = days_ref.shape[0]
    weights = []
    for k in range(-2, 3):
        other = days_ref[wrapped(date + k, count)]
        gap = other - days_ref[date] if k >= 0 else days_ref[date] - other
        gap = jnp.where(gap < 0, gap + cycle_days, gap)
        weights.append(jnp.maximum(8 - gap, 0).astype(jnp.float32))
    total = weights[0] + weights[1] + weights[2] + weights[3] + weights[4]
    return weights, 1.0 / jnp.full((TILE, LANES), total, jnp.float32)


def smoothed_leads(leads, value):
    before, here = None, value(0)
    for lead in range(leads):
        after = value(lead + 1) if lead + 1 < leads else None
        total = here + here
        for beside in (before, after):
            if beside is not None:
                total = total + beside
        yield lead, total * (1.0 / 3.0 if before is None or after is None else 0.25)
        before, here = here, after


def smooth_kernel(
    leads, places, rows, total_rows, members, cycle_days, count, extra, date_ref, days_ref, *refs
):
    sums, (done, sem) = refs[:count], refs[-2:]
    if extra:
        forecast, kept, given = refs[count : count + 3]
        out_hbm, anomalies, weeks, weeks_sem = refs[-6:-2]
        weeks[:, 0, :] = forecast[...] - (kept[...] + given[...])
        copies = [pltpu.make_async_copy(weeks, anomalies, weeks_sem)]
        copies[0].start()
    else:
        out_hbm, copies = refs[-3], []

    def tile(row, lead):
        which, place = places[row]
        start = (place * leads + lead) * TILE
        return sums[which][start : start + TILE, :]

    for slot, row in enumerate(rows):
        weights, inverse = neighbour_weights(days_ref, date_ref[0] * total_rows + row, cycle_days)
        inverse = inverse * (1.0 / members)

        def mean(lead):
            value = weights[0] * tile(row - 2, lead)
            for k in range(1, 5):
                value = value + weights[k] * tile(row - 2 + k, lead)
            return value * inverse

        for lead, value in smoothed_leads(leads, mean):
            done[slot, lead * TILE : (lead + 1) * TILE, :] = value
        copy = pltpu.make_async_copy(done.at[slot], out_hbm.at[row], sem.at[slot])
        copy.start()
        copies.append(copy)
    for copy in copies:
        copy.wait()


def smooth_rows(
    date, days, arrays, rows, total_rows, leads, members, cycle_days, cost, extra=(), into=None
):
    places = {row: (i, j) for i, (_, held) in enumerate(arrays) for j, row in enumerate(held)}
    sums = [array for array, _ in arrays]
    operands = [date, days, *sums, *extra] + ([] if into is None else [into])
    shapes = [jax.ShapeDtypeStruct((total_rows, leads * TILE, LANES), jnp.float32)]
    if extra:
        shapes.append(jax.ShapeDtypeStruct((WEEKS, 1, LANES), jnp.float32))
    return pl.pallas_call(
        functools.partial(
            smooth_kernel, leads, places, rows, total_rows, members, cycle_days, len(sums), bool(extra)
        ),
        in_specs=[SMEM, SMEM]
        + [VMEM] * (len(sums) + len(extra))
        + ([] if into is None else [HBM]),
        out_specs=[HBM] * len(shapes),
        out_shape=shapes,
        scratch_shapes=(
            [pltpu.VMEM((WEEKS, 1, LANES), jnp.float32), pltpu.SemaphoreType.DMA] if extra else []
        )
        + [
            pltpu.VMEM((len(rows), leads * TILE, LANES), jnp.float32),
            pltpu.SemaphoreType.DMA((len(rows),)),
        ],
        input_output_aliases={} if into is None else {len(operands) - 1: 0},
        cost_estimate=estimate(cost),
        compiler_params=pltpu.CompilerParams(vmem_limit_bytes=8 * MIB),
    )(*operands)


def count_weeks(leads, bins_ref, counts):
    for week in range(WEEKS):
        counts[week] = 0
    for lead in range(leads):
        counts[bins_ref[lead]] += 1


def weekly_kernel(
    kinds, leads, rows, members, cycle_days, ens_ref, date_ref, days_ref, position_ref, bins_ref, *refs
):
    runs_ref, give, keep, climate, near, sem, weekly, counts = refs
    group = TILE * kinds
    block = leads * group
    position = position_ref[0]
    dates = days_ref.shape[0]
    row_of = [wrapped(position + k - 2, dates) - date_ref[0] * rows for k in range(5)]
    here = [(row >= 0) & (row < rows) for row in row_of]

    def copy_of(k):
        start = pl.multiple_of(row_of[k] * block, 16)
        return pltpu.make_async_copy(runs_ref.at[pl.ds(start, block)], near.at[k], sem.at[k])

    for k in range(5):

        @pl.when(here[k])
        def _():
            copy_of(k).start()

    weights, inverse = neighbour_weights(days_ref, position, cycle_days)
    inverse = inverse * (1.0 / members)
    count_weeks(leads, bins_ref, counts)
    weekly[...] = jnp.zeros_like(weekly)

    @pl.when(here[0] | here[1] | here[2] | here[3] | here[4])
    def _():
        climate[...] = jnp.zeros_like(climate)
        for k in range(5):

            @pl.when(here[k])
            def _():
                copy_of(k).wait()
                climate[...] += weights[k] * near[k].astype(jnp.float32)

        def part(lead):
            return climate[lead * group : (lead + 1) * group, :]

        for lead, value in smoothed_leads(leads, part):
            span = pl.ds(pl.multiple_of(bins_ref[lead] * group, group), group)
            weekly[span, :] += value

    core, half = ens_ref[0] % 2, ens_ref[0] // 2
    for week in range(WEEKS):
        scale = inverse / jnp.full((TILE, LANES), counts[week].astype(jnp.float32))
        for role, of_half in enumerate((1 - half, half)):
            for out, of_core in ((give, 1 - core), (keep, core)):
                kind = 2 * of_half + of_core
                mean = weekly[pl.ds(week * group + kind, TILE, stride=kinds), :] * scale
                for slot in range(TILE):
                    out[role * TILE + slot, week, :] = mean[slot]


def weekly_shares(ens, date, days, position, bins, flat, kinds, leads, rows, members, cycle_days):
    block = leads * TILE * kinds
    shape = pltpu.VMEM((2 * TILE, WEEKS, LANES), jnp.float32)
    return pl.pallas_call(
        functools.partial(weekly_kernel, kinds, leads, rows, members, cycle_days),
        in_specs=[SMEM] * 5 + [HBM],
        out_specs=[VMEM] * 2,
        out_shape=[shape] * 2,
        scratch_shapes=[
            pltpu.VMEM((block, LANES), jnp.float32),
            pltpu.VMEM((5, block, LANES), jnp.bfloat16),
            pltpu.SemaphoreType.DMA((5,)),
            pltpu.VMEM((WEEKS * TILE * kinds, LANES), jnp.float32),
            pltpu.SMEM((WEEKS,), jnp.int32),
        ],
        cost_estimate=estimate(1),
        compiler_params=pltpu.CompilerParams(vmem_limit_bytes=8 * MIB),
    )(ens, date, days, position, bins, pltpu.with_memory_space_constraint(flat, pltpu.HBM))


def forecast_kernel(leads, bins_ref, forecast_ref, out, total, means, counts):
    count_weeks(leads, bins_ref, counts)
    runs = forecast_ref.shape[0]
    value = forecast_ref[0].astype(jnp.float32)
    for run in range(1, runs):
        value = value + forecast_ref[run].astype(jnp.float32)
    total[...] = value
    means[...] = jnp.zeros_like(means)
    for lead in range(leads):
        means[pl.ds(bins_ref[lead], 1), :] += total[lead : lead + 1, :]
    for week in range(WEEKS):
        count = jnp.full((1, LANES), (counts[week] * runs).astype(jnp.float32))
        out[week : week + 1, :] = means[week : week + 1, :] / count


def forecast_weeks(bins, forecast, leads):
    return pl.pallas_call(
        functools.partial(forecast_kernel, leads),
        in_specs=[SMEM, VMEM],
        out_specs=VMEM,
        out_shape=jax.ShapeDtypeStruct((WEEKS, LANES), jnp.float32),
        scratch_shapes=[
            pltpu.VMEM((leads, LANES), jnp.float32),
            pltpu.VMEM((TILE, LANES), jnp.float32),
            pltpu.SMEM((WEEKS,), jnp.int32),
        ],
        cost_estimate=estimate(1),
        compiler_params=pltpu.CompilerParams(vmem_limit_bytes=4 * MIB),
    )(bins, forecast)


def date_bits():
    slot = lax.axis_index("date").astype(jnp.uint32)
    steps = [1 << bit for bit in range(lax.axis_size("date").bit_length() - 1)][::-1]
    return [number for step in steps for number in ((slot // step) & 1, ((slot // step) & 1) ^ 1)]


def weeks_over_dates(total, bits):
    slots = lax.axis_size("date")
    step = slots // 2
    for mine, other in zip(bits[::2], bits[1::2]):
        halves = total.reshape(2, step, *total.shape[1:])
        give = lax.dynamic_index_in_dim(halves, other, 0, keepdims=False)
        keep = lax.dynamic_index_in_dim(halves, mine, 0, keepdims=False)
        got = lax.ppermute(give, "date", [(i, i ^ step) for i in range(slots)])
        total = keep + got
        step //= 2
    return keep[0], got[0]


def per_device(
    hindcast_runs,
    init_calendar_ordinal,
    prediction_init_position,
    horizon_sevenfold_bin,
    prediction_runs,
):
    _, rows, kinds, leads, cells = hindcast_runs.shape
    dates = rows * lax.axis_size("date")
    members = lax.axis_size("ens")
    cycle_days = 7 * dates // 2
    block = leads * TILE
    ens = lax.axis_index("ens").astype(jnp.int32).reshape(1)
    date = lax.axis_index("date").astype(jnp.int32).reshape(1)

    numbers = date_bits()

    flat = hindcast_runs.reshape(rows, kinds, leads, TILE, LANES)
    flat = flat.transpose(0, 2, 3, 1, 4).reshape(rows * leads * TILE * kinds, LANES)
    flat, ens, date, *numbers = lax.optimization_barrier((flat, ens, date, *numbers))

    first = [0, 1, rows - 2, rows - 1]
    second = list(range(2, rows - 2))
    split = functools.partial(split_kinds, kinds=kinds, leads=leads)

    def for_x(flat, members):
        return split(flat, ens, rows=members, wanted=[(members, True, True), (members, True, False)])

    def pair_sum(mine, other):
        return ((mine.astype(jnp.float32) + other.astype(jnp.float32)) * SCALE).astype(jnp.float16)

    theirs_0, mine_0 = for_x(flat, first)
    got_0 = core_swap(theirs_0)
    flat, mine_0 = lax.optimization_barrier((flat, mine_0))
    theirs_1, mine_1 = for_x(flat, second)
    got_1 = core_swap(theirs_1)
    flat, mine_1 = lax.optimization_barrier((flat, mine_1))
    weeks_give, weeks_keep = weekly_shares(
        ens,
        date,
        init_calendar_ordinal,
        prediction_init_position,
        horizon_sevenfold_bin,
        flat,
        kinds,
        leads,
        rows,
        members,
        cycle_days,
    )
    mine_0, weeks_keep = lax.optimization_barrier((mine_0, weeks_keep))
    packed_0 = pair_sum(mine_0, got_0)
    packed_0, weeks_give = lax.optimization_barrier((packed_0, weeks_give))
    weeks_got = core_swap(weeks_give)
    arrived_0 = chip_swap(packed_0)
    flat, packed_0, mine_1 = lax.optimization_barrier((flat, packed_0, mine_1))
    packed_1 = pair_sum(mine_1, got_1)
    arrived_1 = chip_swap(packed_1)
    parts = [first, second]
    own = split(
        flat,
        ens,
        rows=first + second,
        wanted=[(part, False, other) for part in parts for other in (True, False)],
    )
    others = [core_swap(theirs) for theirs in own[::2]]

    weeks = weeks_keep + weeks_got
    weeks = weeks[TILE:] + chip_swap(weeks[:TILE])
    def local_sum(own, other, own_place, packed, place, count):
        own_span = slice(own_place * block, (own_place + count) * block)
        pair = own[own_span].astype(jnp.float32) + other[own_span].astype(jnp.float32)
        span = slice(place * block, (place + count) * block)
        return pair + packed[span].astype(jnp.float32) * (1.0 / SCALE)

    low = local_sum(own[1], others[0], 0, arrived_0, 0, 2)
    high = local_sum(own[1], others[0], 2, arrived_0, 2, 2)
    bins, low, high = lax.optimization_barrier((horizon_sevenfold_bin, low, high))
    forecast = forecast_weeks(bins, prediction_runs[:, 0], leads)
    weeks, forecast = lax.optimization_barrier((weeks, forecast))
    kept, given = weeks_over_dates(weeks, numbers)
    below = date_shift(high, 1)
    above = date_shift(low, -1)
    middle = local_sum(own[3], others[1], 0, arrived_1, 0, len(second))


    arrays = [
        (below, [-2, -1]),
        (low, [0, 1]),
        (middle, second),
        (high, [rows - 2, rows - 1]),
        (above, [rows, rows + 1]),
    ]
    smooth = functools.partial(
        smooth_rows,
        date,
        init_calendar_ordinal,
        total_rows=rows,
        leads=leads,
        members=members,
        cycle_days=cycle_days,
    )
    [smoothed] = smooth(arrays[1:-1], list(range(2, rows - 2)), cost=10 * MIB)
    smoothed, anomalies = smooth(
        arrays, [0, 1, rows - 2, rows - 1], cost=1, extra=(forecast, kept, given), into=smoothed
    )
    return smoothed.reshape(rows, 1, leads, cells), anomalies


def solution(mesh):
    return jax.shard_map(
        per_device,
        mesh=mesh,
        in_specs=(
            P("ens", "date", None, None, "pix"),
            P(),
            P(),
            P(),
            P(None, "ens", None, ("pix", "date")),
        ),
        out_specs=(P("date", "ens", None, "pix"), P(None, "ens", ("pix", "date"))),
        check_vma=False,
    )
```

```python
import functools

import jax
import jax.numpy as jnp
from jax import lax
from jax.experimental import pallas as pl
from jax.experimental.pallas import tpu as pltpu
from jax.sharding import PartitionSpec as P

WEEKS = 7
LANES = 128
TILE = 8
SCALE = 512.0
MIB = 1024 * 1024
SMEM = pl.BlockSpec(memory_space=pltpu.SMEM)
VMEM = pl.BlockSpec(memory_space=pltpu.VMEM)
HBM = pl.BlockSpec(memory_space=pltpu.HBM)


def estimate(num_bytes):
    return pl.CostEstimate(flops=1, transcendentals=0, bytes_accessed=num_bytes)


def core_swap(block):
    return lax.ppermute(block, "ens", [(0, 1), (1, 0), (2, 3), (3, 2)])


def chip_swap(block):
    return lax.ppermute(block, "ens", [(0, 2), (1, 3), (2, 0), (3, 1)])


def date_shift(block, step):
    count = lax.axis_size("date")
    return lax.ppermute(block, "date", [(i, (i + step) % count) for i in range(count)])


def split_rows(kinds, leads, rows, wanted, ens_ref, copies, held, wide, outs):
    block = leads * TILE
    core, half = ens_ref[0] % 2, ens_ref[0] // 2
    for slot, row in enumerate(rows):
        copies[slot].wait()
        spread = wide.at[slot % 2]
        spread[...] = held[slot].astype(jnp.float32)
        for out, (members, other_half, other_core) in zip(outs, wanted):
            if row not in members:
                continue
            kind = 2 * (1 - half if other_half else half) + (1 - core if other_core else core)
            start = members.index(row) * block
            for lead in range(0, leads, 2):
                picked = spread[pl.ds(lead * TILE * kinds + kind, 2 * TILE, stride=kinds), :]
                out[start + lead * TILE : start + (lead + 2) * TILE, :] = picked.astype(
                    jnp.bfloat16
                )


def start_rows(rows, block, runs_ref, held, sem):
    copies = []
    for slot, row in enumerate(rows):
        copy = pltpu.make_async_copy(
            runs_ref.at[pl.ds(row * block, block)], held.at[slot], sem.at[slot]
        )
        copy.start()
        copies.append(copy)
    return copies


def split_kernel(kinds, leads, rows, wanted, ens_ref, runs_ref, *rest):
    outs, (held, wide, sem) = rest[:-3], rest[-3:]
    copies = start_rows(rows, leads * TILE * kinds, runs_ref, held, sem)
    split_rows(kinds, leads, rows, wanted, ens_ref, copies, held, wide, outs)


def split_scratch(rows, block):
    return [
        pltpu.VMEM((len(rows), block, LANES), jnp.bfloat16),
        pltpu.VMEM((2, block, LANES), jnp.float32),
        pltpu.SemaphoreType.DMA((len(rows),)),
    ]


def split_kinds(flat, ens, kinds, leads, rows, wanted):
    block = leads * TILE
    shapes = [pltpu.VMEM((len(members) * block, LANES), jnp.bfloat16) for members, _, _ in wanted]
    outs = pl.pallas_call(
        functools.partial(split_kernel, kinds, leads, rows, wanted),
        in_specs=[SMEM, HBM],
        out_specs=[VMEM] * len(shapes),
        scratch_shapes=split_scratch(rows, block * kinds),
        out_shape=shapes,
        cost_estimate=estimate(len(rows) * block * LANES * 2 * kinds),
        compiler_params=pltpu.CompilerParams(vmem_limit_bytes=10 * MIB),
    )(ens, pltpu.with_memory_space_constraint(flat, pltpu.HBM))
    return list(outs)


def wrapped(index, count):
    index = jnp.where(index < 0, index + count, index)
    return jnp.where(index >= count, index - count, index)


def neighbour_weights(days_ref, date, cycle_days):
    count = days_ref.shape[0]
    weights = []
    for k in range(-2, 3):
        other = days_ref[wrapped(date + k, count)]
        gap = other - days_ref[date] if k >= 0 else days_ref[date] - other
        gap = jnp.where(gap < 0, gap + cycle_days, gap)
        weights.append(jnp.maximum(8 - gap, 0).astype(jnp.float32))
    total = weights[0] + weights[1] + weights[2] + weights[3] + weights[4]
    return weights, 1.0 / jnp.full((TILE, LANES), total, jnp.float32)


def smoothed_leads(leads, value):
    before, here = None, value(0)
    for lead in range(leads):
        after = value(lead + 1) if lead + 1 < leads else None
        total = here + here
        for beside in (before, after):
            if beside is not None:
                total = total + beside
        yield lead, total * (1.0 / 3.0 if before is None or after is None else 0.25)
        before, here = here, after


def smooth_kernel(
    leads, places, rows, total_rows, members, cycle_days, count, extra, date_ref, days_ref, *refs
):
    sums, (done, sem) = refs[:count], refs[-2:]
    if extra:
        forecast, kept, given = refs[count : count + 3]
        out_hbm, anomalies, weeks, weeks_sem = refs[-6:-2]
        weeks[:, 0, :] = forecast[...] - (kept[...] + given[...])
        copies = [pltpu.make_async_copy(weeks, anomalies, weeks_sem)]
        copies[0].start()
    else:
        out_hbm, copies = refs[-3], []

    def tile(row, lead):
        which, place = places[row]
        start = (place * leads + lead) * TILE
        return sums[which][start : start + TILE, :]

    for slot, row in enumerate(rows):
        weights, inverse = neighbour_weights(days_ref, date_ref[0] * total_rows + row, cycle_days)
        inverse = inverse * (1.0 / members)

        def mean(lead):
            value = weights[0] * tile(row - 2, lead)
            for k in range(1, 5):
                value = value + weights[k] * tile(row - 2 + k, lead)
            return value * inverse

        for lead, value in smoothed_leads(leads, mean):
            done[slot, lead * TILE : (lead + 1) * TILE, :] = value
        copy = pltpu.make_async_copy(done.at[slot], out_hbm.at[row], sem.at[slot])
        copy.start()
        copies.append(copy)
    for copy in copies:
        copy.wait()


def smooth_rows(
    date, days, arrays, rows, total_rows, leads, members, cycle_days, cost, extra=(), into=None
):
    places = {row: (i, j) for i, (_, held) in enumerate(arrays) for j, row in enumerate(held)}
    sums = [array for array, _ in arrays]
    operands = [date, days, *sums, *extra] + ([] if into is None else [into])
    shapes = [jax.ShapeDtypeStruct((total_rows, leads * TILE, LANES), jnp.float32)]
    if extra:
        shapes.append(jax.ShapeDtypeStruct((WEEKS, 1, LANES), jnp.float32))
    return pl.pallas_call(
        functools.partial(
            smooth_kernel, leads, places, rows, total_rows, members, cycle_days, len(sums), bool(extra)
        ),
        in_specs=[SMEM, SMEM]
        + [VMEM] * (len(sums) + len(extra))
        + ([] if into is None else [HBM]),
        out_specs=[HBM] * len(shapes),
        out_shape=shapes,
        scratch_shapes=(
            [pltpu.VMEM((WEEKS, 1, LANES), jnp.float32), pltpu.SemaphoreType.DMA] if extra else []
        )
        + [
            pltpu.VMEM((len(rows), leads * TILE, LANES), jnp.float32),
            pltpu.SemaphoreType.DMA((len(rows),)),
        ],
        input_output_aliases={} if into is None else {len(operands) - 1: 0},
        cost_estimate=estimate(cost),
        compiler_params=pltpu.CompilerParams(vmem_limit_bytes=8 * MIB),
    )(*operands)


def count_weeks(leads, bins_ref, counts):
    for week in range(WEEKS):
        counts[week] = 0
    for lead in range(leads):
        counts[bins_ref[lead]] += 1


def weekly_kernel(
    kinds, leads, rows, members, cycle_days, ens_ref, date_ref, days_ref, position_ref, bins_ref, *refs
):
    runs_ref, give, keep, climate, near, sem, weekly, counts = refs
    group = TILE * kinds
    block = leads * group
    position = position_ref[0]
    dates = days_ref.shape[0]
    row_of = [wrapped(position + k - 2, dates) - date_ref[0] * rows for k in range(5)]
    here = [(row >= 0) & (row < rows) for row in row_of]

    def copy_of(k):
        start = pl.multiple_of(row_of[k] * block, 16)
        return pltpu.make_async_copy(runs_ref.at[pl.ds(start, block)], near.at[k], sem.at[k])

    for k in range(5):

        @pl.when(here[k])
        def _():
            copy_of(k).start()

    weights, inverse = neighbour_weights(days_ref, position, cycle_days)
    inverse = inverse * (1.0 / members)
    count_weeks(leads, bins_ref, counts)
    weekly[...] = jnp.zeros_like(weekly)

    @pl.when(here[0] | here[1] | here[2] | here[3] | here[4])
    def _():
        climate[...] = jnp.zeros_like(climate)
        for k in range(5):

            @pl.when(here[k])
            def _():
                copy_of(k).wait()
                climate[...] += weights[k] * near[k].astype(jnp.float32)

        def part(lead):
            return climate[lead * group : (lead + 1) * group, :]

        for lead, value in smoothed_leads(leads, part):
            span = pl.ds(pl.multiple_of(bins_ref[lead] * group, group), group)
            weekly[span, :] += value

    core, half = ens_ref[0] % 2, ens_ref[0] // 2
    for week in range(WEEKS):
        scale = inverse / jnp.full((TILE, LANES), counts[week].astype(jnp.float32))
        for role, of_half in enumerate((1 - half, half)):
            for out, of_core in ((give, 1 - core), (keep, core)):
                kind = 2 * of_half + of_core
                mean = weekly[pl.ds(week * group + kind, TILE, stride=kinds), :] * scale
                for slot in range(TILE):
                    out[role * TILE + slot, week, :] = mean[slot]


def weekly_shares(ens, date, days, position, bins, flat, kinds, leads, rows, members, cycle_days):
    block = leads * TILE * kinds
    shape = pltpu.VMEM((2 * TILE, WEEKS, LANES), jnp.float32)
    return pl.pallas_call(
        functools.partial(weekly_kernel, kinds, leads, rows, members, cycle_days),
        in_specs=[SMEM] * 5 + [HBM],
        out_specs=[VMEM] * 2,
        out_shape=[shape] * 2,
        scratch_shapes=[
            pltpu.VMEM((block, LANES), jnp.float32),
            pltpu.VMEM((5, block, LANES), jnp.bfloat16),
            pltpu.SemaphoreType.DMA((5,)),
            pltpu.VMEM((WEEKS * TILE * kinds, LANES), jnp.float32),
            pltpu.SMEM((WEEKS,), jnp.int32),
        ],
        cost_estimate=estimate(1),
        compiler_params=pltpu.CompilerParams(vmem_limit_bytes=8 * MIB),
    )(ens, date, days, position, bins, pltpu.with_memory_space_constraint(flat, pltpu.HBM))


def forecast_kernel(leads, bins_ref, forecast_ref, out, total, means, counts):
    count_weeks(leads, bins_ref, counts)
    runs = forecast_ref.shape[0]
    value = forecast_ref[0].astype(jnp.float32)
    for run in range(1, runs):
        value = value + forecast_ref[run].astype(jnp.float32)
    total[...] = value
    means[...] = jnp.zeros_like(means)
    for lead in range(leads):
        means[pl.ds(bins_ref[lead], 1), :] += total[lead : lead + 1, :]
    for week in range(WEEKS):
        count = jnp.full((1, LANES), (counts[week] * runs).astype(jnp.float32))
        out[week : week + 1, :] = means[week : week + 1, :] / count


def forecast_weeks(bins, forecast, leads):
    return pl.pallas_call(
        functools.partial(forecast_kernel, leads),
        in_specs=[SMEM, VMEM],
        out_specs=VMEM,
        out_shape=jax.ShapeDtypeStruct((WEEKS, LANES), jnp.float32),
        scratch_shapes=[
            pltpu.VMEM((leads, LANES), jnp.float32),
            pltpu.VMEM((TILE, LANES), jnp.float32),
            pltpu.SMEM((WEEKS,), jnp.int32),
        ],
        cost_estimate=estimate(1),
        compiler_params=pltpu.CompilerParams(vmem_limit_bytes=4 * MIB),
    )(bins, forecast)


def date_bits():
    slot = lax.axis_index("date").astype(jnp.uint32)
    steps = [1 << bit for bit in range(lax.axis_size("date").bit_length() - 1)][::-1]
    return [number for step in steps for number in ((slot // step) & 1, ((slot // step) & 1) ^ 1)]


def weeks_over_dates(total, bits):
    slots = lax.axis_size("date")
    step = slots // 2
    for mine, other in zip(bits[::2], bits[1::2]):
        halves = total.reshape(2, step, *total.shape[1:])
        give = lax.dynamic_index_in_dim(halves, other, 0, keepdims=False)
        keep = lax.dynamic_index_in_dim(halves, mine, 0, keepdims=False)
        got = lax.ppermute(give, "date", [(i, i ^ step) for i in range(slots)])
        total = keep + got
        step //= 2
    return keep[0], got[0]


def per_device(
    hindcast_runs,
    init_calendar_ordinal,
    prediction_init_position,
    horizon_sevenfold_bin,
    prediction_runs,
):
    _, rows, kinds, leads, cells = hindcast_runs.shape
    dates = rows * lax.axis_size("date")
    members = lax.axis_size("ens")
    cycle_days = 7 * dates // 2
    block = leads * TILE
    ens = lax.axis_index("ens").astype(jnp.int32).reshape(1)
    date = lax.axis_index("date").astype(jnp.int32).reshape(1)

    numbers = date_bits()

    flat = hindcast_runs.reshape(rows, kinds, leads, TILE, LANES)
    flat = flat.transpose(0, 2, 3, 1, 4).reshape(rows * leads * TILE * kinds, LANES)
    flat, ens, date, *numbers = lax.optimization_barrier((flat, ens, date, *numbers))

    first = [0, 1, rows - 2, rows - 1]
    second = list(range(2, rows - 2))
    split = functools.partial(split_kinds, kinds=kinds, leads=leads)

    def pair_sum(mine, other):
        return ((mine.astype(jnp.float32) + other.astype(jnp.float32)) * SCALE).astype(jnp.float16)

    theirs_0, mine_0, theirs_1, mine_1 = split(
        flat,
        ens,
        rows=first + second,
        wanted=[(part, True, other) for part in (first, second) for other in (True, False)],
    )
    got_0, got_1 = core_swap(theirs_0), core_swap(theirs_1)
    flat, mine_0, mine_1 = lax.optimization_barrier((flat, mine_0, mine_1))
    weeks_give, weeks_keep = weekly_shares(
        ens,
        date,
        init_calendar_ordinal,
        prediction_init_position,
        horizon_sevenfold_bin,
        flat,
        kinds,
        leads,
        rows,
        members,
        cycle_days,
    )
    mine_0, weeks_keep = lax.optimization_barrier((mine_0, weeks_keep))
    packed_0 = pair_sum(mine_0, got_0)
    packed_0, weeks_give = lax.optimization_barrier((packed_0, weeks_give))
    weeks_got = core_swap(weeks_give)
    arrived_0 = chip_swap(packed_0)
    flat, packed_0, mine_1 = lax.optimization_barrier((flat, packed_0, mine_1))
    packed_1 = pair_sum(mine_1, got_1)
    arrived_1 = chip_swap(packed_1)
    parts = [first, second]
    own = split(
        flat,
        ens,
        rows=first + second,
        wanted=[(part, False, other) for part in parts for other in (True, False)],
    )
    others = [core_swap(theirs) for theirs in own[::2]]

    weeks = weeks_keep + weeks_got
    weeks = weeks[TILE:] + chip_swap(weeks[:TILE])
    def local_sum(own, other, own_place, packed, place, count):
        own_span = slice(own_place * block, (own_place + count) * block)
        pair = own[own_span].astype(jnp.float32) + other[own_span].astype(jnp.float32)
        span = slice(place * block, (place + count) * block)
        return pair + packed[span].astype(jnp.float32) * (1.0 / SCALE)

    low = local_sum(own[1], others[0], 0, arrived_0, 0, 2)
    high = local_sum(own[1], others[0], 2, arrived_0, 2, 2)
    bins, low, high = lax.optimization_barrier((horizon_sevenfold_bin, low, high))
    forecast = forecast_weeks(bins, prediction_runs[:, 0], leads)
    weeks, forecast = lax.optimization_barrier((weeks, forecast))
    kept, given = weeks_over_dates(weeks, numbers)
    below = date_shift(high, 1)
    above = date_shift(low, -1)
    middle = local_sum(own[3], others[1], 0, arrived_1, 0, len(second))


    arrays = [
        (below, [-2, -1]),
        (low, [0, 1]),
        (middle, second),
        (high, [rows - 2, rows - 1]),
        (above, [rows, rows + 1]),
    ]
    smooth = functools.partial(
        smooth_rows,
        date,
        init_calendar_ordinal,
        total_rows=rows,
        leads=leads,
        members=members,
        cycle_days=cycle_days,
    )
    [smoothed] = smooth(arrays[1:-1], list(range(2, rows - 2)), cost=10 * MIB)
    smoothed, anomalies = smooth(
        arrays, [0, 1, rows - 2, rows - 1], cost=1, extra=(forecast, kept, given), into=smoothed
    )
    return smoothed.reshape(rows, 1, leads, cells), anomalies


def solution(mesh):
    return jax.shard_map(
        per_device,
        mesh=mesh,
        in_specs=(
            P("ens", "date", None, None, "pix"),
            P(),
            P(),
            P(),
            P(None, "ens", None, ("pix", "date")),
        ),
        out_specs=(P("date", "ens", None, "pix"), P(None, "ens", ("pix", "date"))),
        check_vma=False,
    )
```

```python
import functools

import jax
import jax.numpy as jnp
from jax import lax
from jax.experimental import pallas as pl
from jax.experimental.pallas import tpu as pltpu
from jax.sharding import PartitionSpec as P

WEEKS = 7
LANES = 128
TILE = 8
SCALE = 512.0
MIB = 1024 * 1024
SMEM = pl.BlockSpec(memory_space=pltpu.SMEM)
VMEM = pl.BlockSpec(memory_space=pltpu.VMEM)
HBM = pl.BlockSpec(memory_space=pltpu.HBM)


def estimate(num_bytes):
    return pl.CostEstimate(flops=1, transcendentals=0, bytes_accessed=num_bytes)


def core_swap(block):
    return lax.ppermute(block, "ens", [(0, 1), (1, 0), (2, 3), (3, 2)])


def chip_swap(block):
    return lax.ppermute(block, "ens", [(0, 2), (1, 3), (2, 0), (3, 1)])


def date_shift(block, step):
    count = lax.axis_size("date")
    return lax.ppermute(block, "date", [(i, (i + step) % count) for i in range(count)])


def split_rows(kinds, leads, rows, wanted, ens_ref, copies, held, wide, outs):
    block = leads * TILE
    core, half = ens_ref[0] % 2, ens_ref[0] // 2
    for slot, row in enumerate(rows):
        copies[slot].wait()
        spread = wide.at[slot % 2]
        spread[...] = held[slot].astype(jnp.float32)
        for out, (members, other_half, other_core) in zip(outs, wanted):
            if row not in members:
                continue
            kind = 2 * (1 - half if other_half else half) + (1 - core if other_core else core)
            start = members.index(row) * block
            for lead in range(0, leads, 2):
                picked = spread[pl.ds(lead * TILE * kinds + kind, 2 * TILE, stride=kinds), :]
                out[start + lead * TILE : start + (lead + 2) * TILE, :] = picked.astype(
                    jnp.bfloat16
                )


def start_rows(rows, block, runs_ref, held, sem):
    copies = []
    for slot, row in enumerate(rows):
        copy = pltpu.make_async_copy(
            runs_ref.at[pl.ds(row * block, block)], held.at[slot], sem.at[slot]
        )
        copy.start()
        copies.append(copy)
    return copies


def split_kernel(kinds, leads, rows, wanted, ens_ref, runs_ref, *rest):
    outs, (held, wide, sem) = rest[:-3], rest[-3:]
    copies = start_rows(rows, leads * TILE * kinds, runs_ref, held, sem)
    split_rows(kinds, leads, rows, wanted, ens_ref, copies, held, wide, outs)


def split_scratch(rows, block):
    return [
        pltpu.VMEM((len(rows), block, LANES), jnp.bfloat16),
        pltpu.VMEM((2, block, LANES), jnp.float32),
        pltpu.SemaphoreType.DMA((len(rows),)),
    ]


def split_kinds(flat, ens, kinds, leads, rows, wanted):
    block = leads * TILE
    shapes = [pltpu.VMEM((len(members) * block, LANES), jnp.bfloat16) for members, _, _ in wanted]
    outs = pl.pallas_call(
        functools.partial(split_kernel, kinds, leads, rows, wanted),
        in_specs=[SMEM, HBM],
        out_specs=[VMEM] * len(shapes),
        scratch_shapes=split_scratch(rows, block * kinds),
        out_shape=shapes,
        cost_estimate=estimate(len(rows) * block * LANES * 2 * kinds),
        compiler_params=pltpu.CompilerParams(vmem_limit_bytes=10 * MIB),
    )(ens, pltpu.with_memory_space_constraint(flat, pltpu.HBM))
    return list(outs)


def wrapped(index, count):
    index = jnp.where(index < 0, index + count, index)
    return jnp.where(index >= count, index - count, index)


def neighbour_weights(days_ref, date, cycle_days):
    count = days_ref.shape[0]
    weights = []
    for k in range(-2, 3):
        other = days_ref[wrapped(date + k, count)]
        gap = other - days_ref[date] if k >= 0 else days_ref[date] - other
        gap = jnp.where(gap < 0, gap + cycle_days, gap)
        weights.append(jnp.maximum(8 - gap, 0).astype(jnp.float32))
    total = weights[0] + weights[1] + weights[2] + weights[3] + weights[4]
    return weights, 1.0 / jnp.full((TILE, LANES), total, jnp.float32)


def smoothed_leads(leads, value):
    before, here = None, value(0)
    for lead in range(leads):
        after = value(lead + 1) if lead + 1 < leads else None
        total = here + here
        for beside in (before, after):
            if beside is not None:
                total = total + beside
        yield lead, total * (1.0 / 3.0 if before is None or after is None else 0.25)
        before, here = here, after


def smooth_kernel(
    leads, places, rows, total_rows, members, cycle_days, count, extra, date_ref, days_ref, *refs
):
    sums, (done, sem) = refs[:count], refs[-2:]
    if extra:
        forecast, kept, given = refs[count : count + 3]
        out_hbm, anomalies, weeks, weeks_sem = refs[-6:-2]
        weeks[:, 0, :] = forecast[...] - (kept[...] + given[...])
        copies = [pltpu.make_async_copy(weeks, anomalies, weeks_sem)]
        copies[0].start()
    else:
        out_hbm, copies = refs[-3], []

    def tile(row, lead):
        which, place = places[row]
        start = (place * leads + lead) * TILE
        return sums[which][start : start + TILE, :]

    for slot, row in enumerate(rows):
        weights, inverse = neighbour_weights(days_ref, date_ref[0] * total_rows + row, cycle_days)
        inverse = inverse * (1.0 / members)

        def mean(lead):
            value = weights[0] * tile(row - 2, lead)
            for k in range(1, 5):
                value = value + weights[k] * tile(row - 2 + k, lead)
            return value * inverse

        for lead, value in smoothed_leads(leads, mean):
            done[slot, lead * TILE : (lead + 1) * TILE, :] = value
        copy = pltpu.make_async_copy(done.at[slot], out_hbm.at[row], sem.at[slot])
        copy.start()
        copies.append(copy)
    for copy in copies:
        copy.wait()


def smooth_rows(
    date, days, arrays, rows, total_rows, leads, members, cycle_days, cost, extra=(), into=None
):
    places = {row: (i, j) for i, (_, held) in enumerate(arrays) for j, row in enumerate(held)}
    sums = [array for array, _ in arrays]
    operands = [date, days, *sums, *extra] + ([] if into is None else [into])
    shapes = [jax.ShapeDtypeStruct((total_rows, leads * TILE, LANES), jnp.float32)]
    if extra:
        shapes.append(jax.ShapeDtypeStruct((WEEKS, 1, LANES), jnp.float32))
    return pl.pallas_call(
        functools.partial(
            smooth_kernel, leads, places, rows, total_rows, members, cycle_days, len(sums), bool(extra)
        ),
        in_specs=[SMEM, SMEM]
        + [VMEM] * (len(sums) + len(extra))
        + ([] if into is None else [HBM]),
        out_specs=[HBM] * len(shapes),
        out_shape=shapes,
        scratch_shapes=(
            [pltpu.VMEM((WEEKS, 1, LANES), jnp.float32), pltpu.SemaphoreType.DMA] if extra else []
        )
        + [
            pltpu.VMEM((len(rows), leads * TILE, LANES), jnp.float32),
            pltpu.SemaphoreType.DMA((len(rows),)),
        ],
        input_output_aliases={} if into is None else {len(operands) - 1: 0},
        cost_estimate=estimate(cost),
        compiler_params=pltpu.CompilerParams(vmem_limit_bytes=8 * MIB),
    )(*operands)


def count_weeks(leads, bins_ref, counts):
    for week in range(WEEKS):
        counts[week] = 0
    for lead in range(leads):
        counts[bins_ref[lead]] += 1


def weekly_kernel(
    kinds, leads, rows, members, cycle_days, ens_ref, date_ref, days_ref, position_ref, bins_ref, *refs
):
    runs_ref, give, keep, climate, near, sem, weekly, counts = refs
    group = TILE * kinds
    block = leads * group
    position = position_ref[0]
    dates = days_ref.shape[0]
    row_of = [wrapped(position + k - 2, dates) - date_ref[0] * rows for k in range(5)]
    here = [(row >= 0) & (row < rows) for row in row_of]

    def copy_of(k):
        start = pl.multiple_of(row_of[k] * block, 16)
        return pltpu.make_async_copy(runs_ref.at[pl.ds(start, block)], near.at[k], sem.at[k])

    for k in range(5):

        @pl.when(here[k])
        def _():
            copy_of(k).start()

    weights, inverse = neighbour_weights(days_ref, position, cycle_days)
    inverse = inverse * (1.0 / members)
    count_weeks(leads, bins_ref, counts)
    weekly[...] = jnp.zeros_like(weekly)

    @pl.when(here[0] | here[1] | here[2] | here[3] | here[4])
    def _():
        climate[...] = jnp.zeros_like(climate)
        for k in range(5):

            @pl.when(here[k])
            def _():
                copy_of(k).wait()
                climate[...] += weights[k] * near[k].astype(jnp.float32)

        def part(lead):
            return climate[lead * group : (lead + 1) * group, :]

        for lead, value in smoothed_leads(leads, part):
            span = pl.ds(pl.multiple_of(bins_ref[lead] * group, group), group)
            weekly[span, :] += value

    core, half = ens_ref[0] % 2, ens_ref[0] // 2
    for week in range(WEEKS):
        scale = inverse / jnp.full((TILE, LANES), counts[week].astype(jnp.float32))
        for role, of_half in enumerate((1 - half, half)):
            for out, of_core in ((give, 1 - core), (keep, core)):
                kind = 2 * of_half + of_core
                mean = weekly[pl.ds(week * group + kind, TILE, stride=kinds), :] * scale
                for slot in range(TILE):
                    out[role * TILE + slot, week, :] = mean[slot]


def weekly_shares(ens, date, days, position, bins, flat, kinds, leads, rows, members, cycle_days):
    block = leads * TILE * kinds
    shape = pltpu.VMEM((2 * TILE, WEEKS, LANES), jnp.float32)
    return pl.pallas_call(
        functools.partial(weekly_kernel, kinds, leads, rows, members, cycle_days),
        in_specs=[SMEM] * 5 + [HBM],
        out_specs=[VMEM] * 2,
        out_shape=[shape] * 2,
        scratch_shapes=[
            pltpu.VMEM((block, LANES), jnp.float32),
            pltpu.VMEM((5, block, LANES), jnp.bfloat16),
            pltpu.SemaphoreType.DMA((5,)),
            pltpu.VMEM((WEEKS * TILE * kinds, LANES), jnp.float32),
            pltpu.SMEM((WEEKS,), jnp.int32),
        ],
        cost_estimate=estimate(1),
        compiler_params=pltpu.CompilerParams(vmem_limit_bytes=8 * MIB),
    )(ens, date, days, position, bins, pltpu.with_memory_space_constraint(flat, pltpu.HBM))


def forecast_kernel(leads, bins_ref, forecast_ref, out, total, means, counts):
    count_weeks(leads, bins_ref, counts)
    runs = forecast_ref.shape[0]
    value = forecast_ref[0].astype(jnp.float32)
    for run in range(1, runs):
        value = value + forecast_ref[run].astype(jnp.float32)
    total[...] = value
    means[...] = jnp.zeros_like(means)
    for lead in range(leads):
        means[pl.ds(bins_ref[lead], 1), :] += total[lead : lead + 1, :]
    for week in range(WEEKS):
        count = jnp.full((1, LANES), (counts[week] * runs).astype(jnp.float32))
        out[week : week + 1, :] = means[week : week + 1, :] / count


def forecast_weeks(bins, forecast, leads):
    return pl.pallas_call(
        functools.partial(forecast_kernel, leads),
        in_specs=[SMEM, VMEM],
        out_specs=VMEM,
        out_shape=jax.ShapeDtypeStruct((WEEKS, LANES), jnp.float32),
        scratch_shapes=[
            pltpu.VMEM((leads, LANES), jnp.float32),
            pltpu.VMEM((TILE, LANES), jnp.float32),
            pltpu.SMEM((WEEKS,), jnp.int32),
        ],
        cost_estimate=estimate(1),
        compiler_params=pltpu.CompilerParams(vmem_limit_bytes=4 * MIB),
    )(bins, forecast)


def date_bits():
    slot = lax.axis_index("date").astype(jnp.uint32)
    steps = [1 << bit for bit in range(lax.axis_size("date").bit_length() - 1)][::-1]
    return [number for step in steps for number in ((slot // step) & 1, ((slot // step) & 1) ^ 1)]


def weeks_over_dates(total, bits):
    slots = lax.axis_size("date")
    step = slots // 2
    for mine, other in zip(bits[::2], bits[1::2]):
        halves = total.reshape(2, step, *total.shape[1:])
        give = lax.dynamic_index_in_dim(halves, other, 0, keepdims=False)
        keep = lax.dynamic_index_in_dim(halves, mine, 0, keepdims=False)
        got = lax.ppermute(give, "date", [(i, i ^ step) for i in range(slots)])
        total = keep + got
        step //= 2
    return keep[0], got[0]


def per_device(
    hindcast_runs,
    init_calendar_ordinal,
    prediction_init_position,
    horizon_sevenfold_bin,
    prediction_runs,
):
    _, rows, kinds, leads, cells = hindcast_runs.shape
    dates = rows * lax.axis_size("date")
    members = lax.axis_size("ens")
    cycle_days = 7 * dates // 2
    block = leads * TILE
    ens = lax.axis_index("ens").astype(jnp.int32).reshape(1)
    date = lax.axis_index("date").astype(jnp.int32).reshape(1)

    numbers = date_bits()

    flat = hindcast_runs.reshape(rows, kinds, leads, TILE, LANES)
    flat = flat.transpose(0, 2, 3, 1, 4).reshape(rows * leads * TILE * kinds, LANES)
    flat, ens, date, *numbers = lax.optimization_barrier((flat, ens, date, *numbers))

    first = [0, 1, rows - 2, rows - 1]
    second = list(range(2, rows - 2))
    split = functools.partial(split_kinds, kinds=kinds, leads=leads)

    def pair_sum(mine, other):
        return ((mine.astype(jnp.float32) + other.astype(jnp.float32)) * SCALE).astype(jnp.float16)

    theirs_0, mine_0, theirs_1, mine_1 = split(
        flat,
        ens,
        rows=first + second,
        wanted=[(part, True, other) for part in (first, second) for other in (True, False)],
    )
    got_0, got_1 = core_swap(theirs_0), core_swap(theirs_1)
    flat, mine_0, mine_1 = lax.optimization_barrier((flat, mine_0, mine_1))
    weeks_give, weeks_keep = weekly_shares(
        ens,
        date,
        init_calendar_ordinal,
        prediction_init_position,
        horizon_sevenfold_bin,
        flat,
        kinds,
        leads,
        rows,
        members,
        cycle_days,
    )
    packed_0 = pair_sum(mine_0, got_0)
    packed_0, weeks_give = lax.optimization_barrier((packed_0, weeks_give))
    weeks_got = core_swap(weeks_give)
    arrived_0 = chip_swap(packed_0)
    flat, packed_0, mine_1 = lax.optimization_barrier((flat, packed_0, mine_1))
    packed_1 = pair_sum(mine_1, got_1)
    arrived_1 = chip_swap(packed_1)
    parts = [first, second]
    own = split(
        flat,
        ens,
        rows=first + second,
        wanted=[(part, False, other) for part in parts for other in (True, False)],
    )
    others = [core_swap(theirs) for theirs in own[::2]]

    weeks = weeks_keep + weeks_got
    weeks = weeks[TILE:] + chip_swap(weeks[:TILE])
    def local_sum(own, other, own_place, packed, place, count):
        own_span = slice(own_place * block, (own_place + count) * block)
        pair = own[own_span].astype(jnp.float32) + other[own_span].astype(jnp.float32)
        span = slice(place * block, (place + count) * block)
        return pair + packed[span].astype(jnp.float32) * (1.0 / SCALE)

    low = local_sum(own[1], others[0], 0, arrived_0, 0, 2)
    high = local_sum(own[1], others[0], 2, arrived_0, 2, 2)
    bins, low, high = lax.optimization_barrier((horizon_sevenfold_bin, low, high))
    forecast = forecast_weeks(bins, prediction_runs[:, 0], leads)
    weeks, forecast = lax.optimization_barrier((weeks, forecast))
    kept, given = weeks_over_dates(weeks, numbers)
    below = date_shift(high, 1)
    above = date_shift(low, -1)
    middle = local_sum(own[3], others[1], 0, arrived_1, 0, len(second))


    arrays = [
        (below, [-2, -1]),
        (low, [0, 1]),
        (middle, second),
        (high, [rows - 2, rows - 1]),
        (above, [rows, rows + 1]),
    ]
    smooth = functools.partial(
        smooth_rows,
        date,
        init_calendar_ordinal,
        total_rows=rows,
        leads=leads,
        members=members,
        cycle_days=cycle_days,
    )
    [smoothed] = smooth(arrays[1:-1], list(range(2, rows - 2)), cost=10 * MIB)
    smoothed, anomalies = smooth(
        arrays, [0, 1, rows - 2, rows - 1], cost=1, extra=(forecast, kept, given), into=smoothed
    )
    return smoothed.reshape(rows, 1, leads, cells), anomalies


def solution(mesh):
    return jax.shard_map(
        per_device,
        mesh=mesh,
        in_specs=(
            P("ens", "date", None, None, "pix"),
            P(),
            P(),
            P(),
            P(None, "ens", None, ("pix", "date")),
        ),
        out_specs=(P("date", "ens", None, "pix"), P(None, "ens", ("pix", "date"))),
        check_vma=False,
    )
```
